256 devices in a mesh: ops: 128 (over y_hi, x, z, core), sec: 2 (over y_lo).
Axes of the slice: x: 4, y: 4 (y_hi: 2, y_lo: 2; y = y_hi * 2 + y_lo), z: 8, core: 2. Of those that a mesh axis runs over, the one named last changes fastest.
Arguments:
- wavefunction: bfloat16 [8, 512, 512], P('sec'), may hold values from -6 to 6
- left_ops: bfloat16 [128, 512, 512], P('ops'), may hold values from -0.25 to 0.25
- right_ops: bfloat16 [128, 512, 512], P('ops'), may hold values from -0.25 to 0.25
- shift_map: int32 [128], P('ops'), may hold values from 0 to 7
- sector_sizes: int32 [8], replicated, may hold values from 256 to 512, as said below
- step_sizes: int32 [2], replicated, may hold values from 1 to 5
- integrals: float32 [128, 3], P('ops'), may hold values from 0.25 to 1
Outputs:
- final_wave: float32 [8, 512, 512], P('sec')
- mixed_ops: bfloat16 [128, 512, 512], P('ops', None, 'sec')
The draws below stay inside these ranges and needn't reach their ends.
Inputs may be any that keep to these rules, and one draw needn't show every extreme that they name: `sector_sizes`: each sector holds between 256 and 512 states; some sector holds exactly 512.
All inputs are finite; a program needn't handle non-finite values.
Results may differ from the reference program's by a relative error of at most 0.015.
Values may be sent and summed in bfloat16 or wider, within the bound.
A program may use at most 64 MiB of HBM per device.

```python
import jax
import jax.numpy as jnp
from jax import lax

M = 512
S = 8
ITERS = 2
OPERATORS = 128


def draw_sector_sizes(key, part):
    first_key = jax.random.fold_in(key, 11)
    second_key = jax.random.fold_in(key, 23)
    sizes = jax.random.randint(first_key, (S,), M // 2, M + 1).astype(jnp.int32)
    chosen = jax.random.randint(second_key, (), 0, S).astype(jnp.int32)
    return jnp.where(jnp.arange(S, dtype=jnp.int32) == chosen, M, sizes).astype(jnp.int32)


def plant(entries, rng, least, high):
    dims = entries.shape
    place = [jax.random.randint(jax.random.fold_in(rng, axis), (), 0, dims[axis]) for axis in range(len(dims))]
    entries = entries.at[tuple(place)].set(least)
    longest = dims.index(max(dims))
    place[longest] = (place[longest] + 1) % dims[longest]
    return entries.at[tuple(place)].set(high)


def block_scale(key, dims, split, low, largest):
    gain = 1.0
    for axis_at, blocks in split:
        draws = jax.random.uniform(jax.random.fold_in(jax.random.fold_in(key, 6), axis_at), (blocks,), jnp.float32, low / len(split), largest / len(split))
        gain = gain * jnp.repeat(jnp.exp(draws), dims[axis_at] // blocks).reshape((-1,) + (1,) * (len(dims) - 1 - axis_at))
    return gain


def normal_values(key, extent, scale, bound, pieces=(), kind=jnp.bfloat16):
    level = block_scale(key, extent, pieces, -0.22, 0.18) if pieces else 1.0
    entries = jax.random.normal(key, extent, jnp.float32) * scale * level
    return jnp.minimum(jnp.maximum(entries, -bound), bound).astype(kind)


def setup_inputs(seed: int = 0) -> dict:
    key_list = jax.random.split(jax.random.key(seed), 8)
    wavefunction = normal_values(key_list[0], (S, M, M), 1.0, 6.0, ((0, 2),))
    left_ops = normal_values(key_list[1], (OPERATORS, M, M), M ** -0.5, 0.25, ((0, 128),))
    right_ops = normal_values(key_list[2], (OPERATORS, M, M), M ** -0.5, 0.25, ((0, 128),))
    shift_map = plant(jax.random.randint(key_list[3], (OPERATORS,), 0, S), jax.random.fold_in(key_list[3], 1), 0, S - 1).astype(jnp.int32)
    sector_sizes = draw_sector_sizes(jax.random.fold_in(key_list[7], 71), 0)
    step_sizes = jax.random.randint(key_list[5], (ITERS,), 1, 6).astype(jnp.int32)
    integrals = jnp.clip(0.25 + 0.75 * jax.random.uniform(key_list[6], (OPERATORS, 3), jnp.float32) ** block_scale(key_list[6], (OPERATORS, 3), ((0, 128),), -0.2, 0.2), 0.25, 1.0)
    return {"wavefunction": wavefunction, "left_ops": left_ops, "right_ops": right_ops, "shift_map": shift_map, "sector_sizes": sector_sizes, "step_sizes": step_sizes, "integrals": integrals}


def reference(wavefunction, left_ops, right_ops, shift_map, sector_sizes, step_sizes, integrals):
    highest = lax.Precision.HIGHEST
    sectors = wavefunction.shape[0]
    width = wavefunction.shape[1]
    count = left_ops.shape[0]
    column = jnp.arange(width, dtype=jnp.int32)
    row_ok = (column[None, :] < sector_sizes[:, None]).astype(jnp.float32)
    mask = row_ok[:, :, None] * row_ok[:, None, :]
    psi = wavefunction.astype(jnp.float32) * mask
    order = jnp.arange(sectors, dtype=jnp.int32)

    def apply(state):
        state_low = state.astype(jnp.bfloat16).astype(jnp.float32)

        def one(total, member):
            left, right, shift = member
            source = jnp.take(state_low, ((order - shift) % sectors).astype(jnp.int32), axis=0)
            inner = jnp.einsum('mn,snp->smp', left.astype(jnp.float32), source, precision=highest)
            inner = inner.astype(jnp.bfloat16).astype(jnp.float32)
            return (total + jnp.einsum('smp,qp->smq', inner, right.astype(jnp.float32), precision=highest), None)
        total, _ = lax.scan(one, jnp.zeros_like(state), (left_ops, right_ops, shift_map))
        return total
    for step in range(ITERS):
        hpsi = apply(psi)
        factor = step_sizes[step].astype(jnp.float32) / (8.0 * jnp.sqrt(jnp.float32(count)))
        psi = mask * (psi - factor * hpsi)
        total = jnp.sum(psi * psi)
        psi = psi / jnp.sqrt(total / (sectors * width * width) + 1e-06)
    basis = psi[0].astype(jnp.bfloat16).astype(jnp.float32)

    def rotate(left):
        half = jnp.dot(basis.T, left.astype(jnp.float32), precision=highest)
        half = half.astype(jnp.bfloat16).astype(jnp.float32)
        return jnp.dot(half, basis, precision=highest) / width
    rotated = lax.map(rotate, left_ops)
    padded = jnp.pad(rotated, ((1, 1), (0, 0), (0, 0)))
    mixed = integrals[:, 0, None, None] * padded[:-2] + integrals[:, 1, None, None] * padded[1:-1] + integrals[:, 2, None, None] * padded[2:]
    return (psi, mixed.astype(jnp.bfloat16))
```

```python
import functools
import math

import jax
import jax.numpy as jnp
from jax import lax
from jax.experimental import pallas as pl
from jax.experimental.pallas import tpu as pltpu
from jax.sharding import PartitionSpec as P

MESH = pl.DeviceIdType.MESH
F32 = jnp.float32
BF16 = jnp.bfloat16
M = 512
S = 8
OPERATORS = 128
YH, X, Z = 2, 4, 8
G = YH * X
Y = 2 * YH
XY = X * Y
OWNERS = G * Z
HALF = 2 * M
CHUNK = HALF // OWNERS
GROW = HALF // G
ZROW = HALF // Z
LAST = 3


def loop(low, high, body):
    lax.fori_loop(low, high, lambda i, c: (body(i), c)[1], 0)


def rem(a, b):
    return lax.rem(a, jnp.int32(b))


def div(a, b):
    return lax.div(a, jnp.int32(b))


def kernel(
    wave, left, right, shift, sizes, steps, integ,
    psi_out, mixed_out, scale_out,
    psi_a, psi_b, psi_f, right_t, near, lmix, chunk, acc,
    csend, cland, s1, l1, s2, l2, norm,
    pre_s, pre_r, fwd_s, fwd_r, near_s, near_r, c_s, c_r, s1_s, s1_r, s2_s, s2_r,
    ga_s, ga_r, gb_s, gb_r, gc_s, gc_r, ha_s, ha_r, hb_s, hb_r, hc_s, hc_r, n_s, n_r,
):
    ops = lax.axis_index("ops")
    sec = lax.axis_index("sec")
    core = rem(ops, 2)
    z = rem(div(ops, 2), Z)
    x = rem(div(ops, 2 * Z), X)
    yh = div(ops, 2 * Z * X)
    y = yh * 2 + sec
    g = yh * X + x
    first = sec * 4
    other = 1 - sec

    def at(xx, yy, zz, cc):
        return ((div(yy, 2) * X + xx) * Z + zz) * 2 + cc, rem(yy, 2)

    def xy_to(d):
        return rem(x + rem(d, X), X), rem(y + div(d, X), Y)

    def xy_from(d):
        return rem(x - rem(d, X) + X, X), rem(y - div(d, X) + Y, Y)

    def g_to(d):
        return rem(x + rem(d, X), X), rem(yh + div(d, X), YH)

    partner = at(x, y, z, 1 - core)
    up = at(x, rem(y + 1, Y), z, core)
    down = at(x, rem(y + Y - 1, Y), z, core)
    after = (rem(ops + 1, OPERATORS), sec)
    before = (rem(ops + OPERATORS - 1, OPERATORS), sec)

    def copy(src, dst, send, recv, device):
        return pltpu.make_async_remote_copy(
            src_ref=src, dst_ref=dst, send_sem=send, recv_sem=recv, device_id=device, device_id_type=MESH
        )

    barrier = pltpu.get_barrier_semaphore()

    def greet(device):
        pl.semaphore_signal(barrier, inc=1, device_id=device, device_id_type=MESH)

    greet(partner)
    greet(after)
    greet(before)

    def greet_xy(d):
        xx, yy = xy_to(d)
        greet(at(xx, yy, z, core))

    loop(1, XY, greet_xy)
    loop(1, Z, lambda d: greet(at(x, y, rem(z + d, Z), core)))

    row = lax.broadcasted_iota(jnp.int32, (M, 128), 0)
    col = lax.broadcasted_iota(jnp.int32, (M, 128), 1)

    def fill(t):
        size = sizes[first + t]
        for b in range(4):
            ok = (row < size) & (col < size - 128 * b)
            block = wave[t, :, 128 * b : 128 * b + 128].astype(F32)
            psi_a[sec, t, b // 2, pl.ds(b % 2 * M, M), :] = jnp.where(ok, block, 0.0).astype(BF16)

    loop(0, 4, fill)
    pl.semaphore_wait(barrier, 3 + XY - 1 + Z - 1)

    def pre(t, target, owner):
        return copy(
            psi_a.at[owner, t, core], psi_a.at[owner, t, core], pre_s.at[t], pre_r.at[t], target
        )

    for t in (0, 2, 1, 3):
        pre(t, up if t < 2 else down, sec).start()
    near_copies = [
        copy(left.at[0], near.at[0], near_s.at[0], near_r.at[0], after),
        copy(left.at[0], near.at[1], near_s.at[1], near_r.at[1], before),
    ]
    for c in near_copies:
        c.start()
    for h in range(2):
        right_t[h] = right[0, 256 * h : 256 * h + 256, :].T

    def start_chunk(t, o):
        chunk[t] = psi_a[sec, t, core, pl.ds(pl.multiple_of(o * CHUNK, CHUNK), CHUNK), :].astype(F32)

    own = [z * G + g if t == LAST else g * Z + z for t in range(4)]
    for t in range(4):
        start_chunk(t, own[t])

    def forward(t):
        ref = psi_a.at[other, t, core]
        return copy(ref, ref, fwd_s.at[t], fwd_r.at[t], partner)

    for t in (0, 2, 1, 3):
        pre(t, up, other).wait_recv()
        forward(t).start()
    for t in range(4):
        forward(t).wait_recv()

    def rows(o, n):
        return pl.ds(pl.multiple_of(o * n, n), n)

    def core_copy(it, t):
        return copy(csend.at[it, t], cland.at[it, t], c_s.at[it, t], c_r.at[it, t], partner)

    def compute(it, t, psi):
        source = rem(first + t - shift[0] + S, S)
        sa, sb = div(source, 4), rem(source, 4)
        block = jnp.concatenate(
            [psi[sa, sb, b // 2, pl.ds(b % 2 * M, M), :] for b in range(4)], axis=1
        )
        inner = jnp.dot(left[0], block, preferred_element_type=F32).astype(BF16)
        theirs = jnp.dot(inner, right_t[1 - core], preferred_element_type=F32).astype(BF16)
        csend[it, t, pl.ds(0, M), :] = theirs[:, :128]
        csend[it, t, pl.ds(M, M), :] = theirs[:, 128:]
        core_copy(it, t).start()
        mine = jnp.dot(inner, right_t[core], preferred_element_type=F32)
        acc[t, pl.ds(0, M), :] = mine[:, :128]
        acc[t, pl.ds(M, M), :] = mine[:, 128:]

    def s1_copy(it, t, d):
        if t == LAST:
            zz = rem(z + d, Z)
            device, src = at(x, y, zz, core), s1.at[it, t, rows(zz, ZROW)]
        else:
            xx, hh = g_to(d)
            device, src = at(xx, hh * 2 + sec, z, core), s1.at[it, t, rows(hh * X + xx, GROW)]
        return copy(src, l1.at[it, t, d], s1_s.at[it, t, d], s1_r.at[it, t, d], device)

    def s2_copy(it, t, d):
        if t == LAST:
            xx, hh = g_to(d)
            device, src = at(xx, hh * 2 + sec, z, core), s2.at[it, t, rows(hh * X + xx, CHUNK)]
        else:
            zz = rem(z + d, Z)
            device, src = at(x, y, zz, core), s2.at[it, t, rows(zz, CHUNK)]
        return copy(src, l2.at[it, t, d], s2_s.at[it, t, d], s2_r.at[it, t, d], device)

    def scatter(it, t):
        core_copy(it, t).wait_recv()

        def add(b):
            part = rows(b, 128)
            s1[it, t, part, :] = (acc[t, part, :] + cland[it, t, part, :].astype(F32)).astype(BF16)

        loop(0, HALF // 128, add)
        loop(1, 8, lambda d: s1_copy(it, t, d).start())

    def reduce_first(it, t):
        loop(1, 8, lambda d: s1_copy(it, t, d).wait_recv())
        total = s1[it, t, rows(z, ZROW) if t == LAST else rows(g, GROW), :].astype(F32)
        for d in range(1, 8):
            total = total + l1[it, t, d].astype(F32)
        s2[it, t] = total.astype(BF16)
        loop(1, 8, lambda d: s2_copy(it, t, d).start())

    def reduce_second(it, t, target):
        loop(1, 8, lambda d: s2_copy(it, t, d).wait_recv())
        total = s2[it, t, rows(g if t == LAST else z, CHUNK), :].astype(F32)
        for d in range(1, 8):
            total = total + l2[it, t, d].astype(F32)
        size = sizes[first + t]
        start = own[t] * CHUNK
        block = 2 * core + div(start, M)
        r = lax.broadcasted_iota(jnp.int32, (CHUNK, 128), 0) + rem(start, M)
        q = lax.broadcasted_iota(jnp.int32, (CHUNK, 128), 1) + block * 128
        factor = steps[it].astype(F32) * (1.0 / (8.0 * math.sqrt(OPERATORS)))
        value = jnp.where((r < size) & (q < size), chunk[t] - factor * total, 0.0)
        chunk[t] = value
        target[sec, t, core, rows(own[t], CHUNK), :] = value.astype(BF16)

    def step(it, psi, target):
        compute(it, 0, psi)
        compute(it, 1, psi)
        scatter(it, 0)
        compute(it, 2, psi)
        scatter(it, 1)
        compute(it, 3, psi)
        scatter(it, 2)
        scatter(it, 3)
        for t in range(4):
            reduce_first(it, t)
        for t in range(4):
            reduce_second(it, t, target)

    def same(ref, send, recv, device):
        return copy(ref, ref, send, recv, device)

    step(0, psi_a, psi_b)

    def ga(d):
        ref = psi_b.at[sec, pl.ds(0, 3), core, rows(own[0], CHUNK)]
        return same(ref, ga_s.at[0, d], ga_r.at[0, d], at(x, y, rem(z + d, Z), core))

    def gb(d):
        xx, yy = xy_to(d)
        ref = psi_b.at[sec, pl.ds(0, 3), core, rows(g, GROW)]
        return same(ref, gb_s.at[0, d], gb_r.at[0, d], at(xx, yy, z, core))

    def gc(d):
        xx, yy = xy_from(d)
        ref = psi_b.at[rem(yy, 2), pl.ds(0, 3), core, rows(div(yy, 2) * X + xx, GROW)]
        return same(ref, gc_s.at[0, d], gc_r.at[0, d], partner)

    def ha(d):
        xx, yy = xy_to(d)
        ref = psi_b.at[sec, LAST, core, rows(own[LAST], CHUNK)]
        return same(ref, ha_s.at[0, d], ha_r.at[0, d], at(xx, yy, z, core))

    def hb(d):
        ref = psi_b.at[pl.ds(0, 2), LAST, core, rows(z, ZROW)]
        return same(ref, hb_s.at[0, d], hb_r.at[0, d], at(x, y, rem(z + d, Z), core))

    def hc(d):
        ref = psi_b.at[pl.ds(0, 2), LAST, core, rows(rem(z - d + Z, Z), ZROW)]
        return same(ref, hc_s.at[0, d], hc_r.at[0, d], partner)

    loop(1, Z, lambda d: ga(d).start())
    loop(1, XY, lambda d: ha(d).start())
    loop(1, Z, lambda d: ga(d).wait_recv())
    loop(1, XY, lambda d: gb(d).start())
    loop(1, XY, lambda d: ha(d).wait_recv())
    loop(1, Z, lambda d: hb(d).start())
    gc(0).start()
    hc(0).start()

    def pass_g(d):
        gb(d).wait_recv()
        gc(d).start()

    def pass_h(d):
        hb(d).wait_recv()
        hc(d).start()

    loop(1, XY, pass_g)
    loop(1, Z, pass_h)
    loop(0, XY, lambda d: gc(d).wait_recv())
    loop(0, Z, lambda d: hc(d).wait_recv())

    def squares(ref, a, t):
        def add(i, total):
            part = ref[a, t, div(i, 8), rows(rem(i, 8), 128), :].astype(F32)
            return total + jnp.sum((part * part).reshape(16, 8, 128), axis=0)

        return lax.fori_loop(0, 16, add, jnp.zeros((8, 128), F32))

    step(1, psi_b, psi_f)

    def ia(d):
        ref = psi_f.at[sec, pl.ds(0, 3), core, rows(own[0], CHUNK)]
        return same(ref, ga_s.at[1, d], ga_r.at[1, d], at(x, y, rem(z + d, Z), core))

    def ib(d):
        xx, hh = g_to(d)
        ref = psi_f.at[sec, pl.ds(0, 3), core, rows(g, GROW)]
        return same(ref, gb_s.at[1, d], gb_r.at[1, d], at(xx, hh * 2 + sec, z, core))

    def ic(d):
        gg = rem(yh - div(d, X) + YH, YH) * X + rem(x - rem(d, X) + X, X)
        ref = psi_f.at[sec, pl.ds(0, 3), core, rows(gg, GROW)]
        return same(ref, gc_s.at[1, d], gc_r.at[1, d], partner)

    def ja(d):
        xx, hh = g_to(d)
        ref = psi_f.at[sec, LAST, core, rows(own[LAST], CHUNK)]
        return same(ref, ha_s.at[1, d], ha_r.at[1, d], at(xx, hh * 2 + sec, z, core))

    def jb(d):
        ref = psi_f.at[sec, LAST, core, rows(z, ZROW)]
        return same(ref, hb_s.at[1, d], hb_r.at[1, d], at(x, y, rem(z + d, Z), core))

    def jc(d):
        ref = psi_f.at[sec, LAST, core, rows(rem(z - d + Z, Z), ZROW)]
        return same(ref, hc_s.at[1, d], hc_r.at[1, d], partner)

    def basis_to(d):
        xx, hh = g_to(d)
        ref = psi_f.at[0, 0, core, rows(g, GROW)]
        return same(ref, gb_s.at[1, 8 + d], gb_r.at[1, 8 + d], at(xx, hh * 2 + other, z, core))

    def basis_pass(d):
        gg = rem(yh - div(d, X) + YH, YH) * X + rem(x - rem(d, X) + X, X)
        ref = psi_f.at[0, 0, core, rows(gg, GROW)]
        return same(ref, gc_s.at[1, 8 + d], gc_r.at[1, 8 + d], partner)

    loop(1, Z, lambda d: ia(d).start())
    loop(1, G, lambda d: ja(d).start())
    loop(1, Z, lambda d: ia(d).wait_recv())

    @pl.when(sec == 0)
    def _():
        loop(0, G, lambda d: basis_to(d).start())

    loop(1, G, lambda d: ib(d).start())
    loop(1, G, lambda d: ja(d).wait_recv())
    loop(1, Z, lambda d: jb(d).start())
    ic(0).start()
    jc(0).start()

    for c in near_copies:
        c.wait_recv()
    w0 = jnp.where(ops == 0, 0.0, integ[0, 0])
    w1 = integ[0, 1]
    w2 = jnp.where(ops == OPERATORS - 1, 0.0, integ[0, 2])

    def mix(i):
        part = rows(i, 64)
        lmix[part, :] = (
            w0 * near[0, part, :].astype(F32)
            + w1 * left[0, part, :].astype(F32)
            + w2 * near[1, part, :].astype(F32)
        ).astype(BF16)

    loop(0, M // 64, mix)

    total1 = jnp.zeros((8, 128), F32)
    for a in range(2):
        for t in range(4):
            total1 = total1 + squares(psi_b, a, t)

    @pl.when(sec == 1)
    def _():
        def pass_basis(d):
            basis_to(d).wait_recv()
            basis_pass(d).start()

        loop(0, G, pass_basis)

    def pass_i(d):
        ib(d).wait_recv()
        ic(d).start()

    def pass_j(d):
        jb(d).wait_recv()
        jc(d).start()

    loop(1, G, pass_i)
    loop(1, Z, pass_j)

    @pl.when(sec == 1)
    def _():
        loop(0, G, lambda d: basis_pass(d).wait_recv())

    loop(0, G, lambda d: ic(d).wait_recv())
    loop(0, Z, lambda d: jc(d).wait_recv())

    total2 = jnp.zeros((8, 128), F32)
    for t in range(4):
        total2 = total2 + squares(psi_f, sec, t)
    norm[0] = total2
    exchange = copy(norm.at[0], norm.at[1], n_s.at[0], n_r.at[0], at(x, 2 * yh + other, z, core))
    exchange.start()

    psi_out[...] = psi_f[sec]
    basis = jnp.concatenate([psi_f[0, 0, b // 2, pl.ds(b % 2 * M, M), :] for b in range(4)], axis=1)
    basis_cols = jnp.concatenate([psi_f[0, 0, sec, pl.ds(b * M, M), :] for b in range(2)], axis=1)
    half = jnp.dot(lmix[...], basis_cols, preferred_element_type=F32).astype(BF16)
    rotated = lax.dot_general(
        basis, half, (((0,), (0,)), ((), ())), preferred_element_type=F32
    )

    exchange.wait_recv()
    count = float(S * M * M)
    sum1 = jnp.sum(total1, axis=(0, 1), keepdims=True)
    sum2 = jnp.sum(norm[0] + norm[1], axis=(0, 1), keepdims=True)
    square = sum2 * (1.0 / count) + 1e-06 * (sum1 * (1.0 / count) + 1e-06)
    scale = lax.rsqrt(square)
    scale_out[...] = jnp.broadcast_to(scale, (8, 128))
    mixed_out[0] = (rotated * (scale * scale * (1.0 / M))).astype(BF16)

    exchange.wait_send()
    for c in near_copies:
        c.wait_send()
    for t in range(4):
        pre(t, up, sec).wait_send()
        forward(t).wait_send()
    for it in range(2):
        for t in range(4):
            core_copy(it, t).wait_send()
            loop(1, 8, lambda d, it=it, t=t: s1_copy(it, t, d).wait_send())
            loop(1, 8, lambda d, it=it, t=t: s2_copy(it, t, d).wait_send())
    loop(1, Z, lambda d: ga(d).wait_send())
    loop(1, XY, lambda d: gb(d).wait_send())
    loop(0, XY, lambda d: gc(d).wait_send())
    loop(1, XY, lambda d: ha(d).wait_send())
    loop(1, Z, lambda d: hb(d).wait_send())
    loop(0, Z, lambda d: hc(d).wait_send())
    loop(1, Z, lambda d: ia(d).wait_send())
    loop(1, G, lambda d: ib(d).wait_send())
    loop(0, G, lambda d: ic(d).wait_send())
    loop(1, G, lambda d: ja(d).wait_send())
    loop(1, Z, lambda d: jb(d).wait_send())
    loop(0, Z, lambda d: jc(d).wait_send())

    @pl.when(sec == 0)
    def _():
        loop(0, G, lambda d: basis_to(d).wait_send())

    @pl.when(sec == 1)
    def _():
        loop(0, G, lambda d: basis_pass(d).wait_send())


def shards(*args):
    vmem = pl.BlockSpec(memory_space=pltpu.VMEM)
    smem = pl.BlockSpec(memory_space=pltpu.SMEM)
    dma = pltpu.SemaphoreType.DMA
    psi = pltpu.VMEM((2, 4, 2, HALF, 128), BF16)
    raw, mixed, scale = pl.pallas_call(
        kernel,
        out_shape=(
            jax.ShapeDtypeStruct((4, 2, HALF, 128), BF16),
            jax.ShapeDtypeStruct((1, M, M // 2), BF16),
            jax.ShapeDtypeStruct((8, 128), F32),
        ),
        in_specs=[vmem, vmem, vmem, smem, smem, smem, smem],
        out_specs=(vmem, vmem, vmem),
        scratch_shapes=[
            psi,
            psi,
            psi,
            pltpu.VMEM((2, M, 256), BF16),
            pltpu.VMEM((2, M, M), BF16),
            pltpu.VMEM((M, M), BF16),
            pltpu.VMEM((4, CHUNK, 128), F32),
            pltpu.VMEM((4, HALF, 128), F32),
            pltpu.VMEM((2, 4, HALF, 128), BF16),
            pltpu.VMEM((2, 4, HALF, 128), BF16),
            pltpu.VMEM((2, 4, HALF, 128), BF16),
            pltpu.VMEM((2, 4, 8, GROW, 128), BF16),
            pltpu.VMEM((2, 4, GROW, 128), BF16),
            pltpu.VMEM((2, 4, 8, CHUNK, 128), BF16),
            pltpu.VMEM((2, 8, 128), F32),
            dma((4,)), dma((4,)), dma((4,)), dma((4,)), dma((2,)), dma((2,)),
            dma((2, 4)), dma((2, 4)), dma((2, 4, 8)), dma((2, 4, 8)), dma((2, 4, 8)), dma((2, 4, 8)),
            dma((2, Z)), dma((2, Z)), dma((2, XY)), dma((2, XY)), dma((2, XY)), dma((2, XY)),
            dma((2, XY)), dma((2, XY)), dma((2, Z)), dma((2, Z)), dma((2, Z)), dma((2, Z)),
            dma((1,)), dma((1,)),
        ],
        compiler_params=pltpu.CompilerParams(
            collective_id=0, has_side_effects=True, vmem_limit_bytes=60 * 2**20
        ),
        name="dmrg_window",
    )(*args)
    wave = raw.reshape(4, 4, M, 128).transpose(0, 2, 1, 3).reshape(4, M, M)
    return wave.astype(F32) * scale[0, 0], mixed


def solution(mesh):
    placed = (
        P("sec", None, None),
        P("ops", None, None),
        P("ops", None, None),
        P("ops"),
        P(),
        P(),
        P("ops", None),
    )
    return jax.shard_map(
        shards,
        mesh=mesh,
        in_specs=placed,
        out_specs=(P("sec", None, None), P("ops", None, "sec")),
        check_vma=False,
    )
```

```python
import math

import jax
import jax.numpy as jnp
from jax import lax
from jax.experimental import pallas as pl
from jax.experimental.pallas import tpu as pltpu
from jax.sharding import PartitionSpec as P

MESH = pl.DeviceIdType.MESH
F32 = jnp.float32
BF16 = jnp.bfloat16
M = 512
S = 8
OPERATORS = 128
YH, X, Z = 2, 4, 8
G = YH * X
Y = 2 * YH
XY = X * Y
HALF = 2 * M
CHUNK = HALF // (G * Z)
BLOCK = HALF // 8
LAST = 3
ORDER = (3, 0, 1, 2)


def loop(low, high, body):
    lax.fori_loop(low, high, lambda i, c: (body(i), c)[1], 0)


def rem(a, b):
    return lax.rem(a, jnp.int32(b))


def div(a, b):
    return lax.div(a, jnp.int32(b))


def rows(o, n):
    return pl.ds(pl.multiple_of(o * n, n), n)


def kernel(
    wave, left, right, shift, sizes, steps, integ,
    psi_out, mixed_out, scale_out,
    psi, bas, right_t, near, lmix, chunk, give, acc,
    csend, cland, s1, l1, l1z, s2, s2z, l2, l2z, nz, nxy, nc, total, rotated,
    near_s, near_r, c_s, c_r, s1_s, s1_r, s2_s, s2_r, a_s, a_r, b_s, b_r, f_s, f_r, bas_s, bas_r, n_s, n_r,
):
    ops = lax.axis_index("ops")
    sec = lax.axis_index("sec")
    core = rem(ops, 2)
    z = rem(div(ops, 2), Z)
    x = rem(div(ops, 2 * Z), X)
    yh = div(ops, 2 * Z * X)
    y = yh * 2 + sec
    g = yh * X + x
    first = sec * 4

    def at(xx, yy, zz, cc):
        return ((div(yy, 2) * X + xx) * Z + zz) * 2 + cc, rem(yy, 2)

    def xy_to(d):
        return rem(x + rem(d, X), X), rem(y + div(d, X), Y)

    def g_to(d):
        return rem(x + rem(d, X), X), rem(y + 2 * div(d, X), Y)

    partner = at(x, y, z, 1 - core)
    after = (rem(ops + 1, OPERATORS), sec)
    before = (rem(ops + OPERATORS - 1, OPERATORS), sec)

    def copy(src, dst, send, recv, device):
        return pltpu.make_async_remote_copy(
            src_ref=src, dst_ref=dst, send_sem=send, recv_sem=recv, device_id=device, device_id_type=MESH
        )

    sent = []

    def start(made):
        made.start()
        sent.append(made.wait_send)

    def group(low, high, make, whole, send, recv):
        loop(low, high, lambda d: make(d).start())
        sent.append(copy(whole, whole, send, recv, partner).wait_send)

    def arrived(whole, send, recv):
        copy(whole, whole, send, recv, partner).wait_recv()

    barrier = pltpu.get_barrier_semaphore()

    def greet(device):
        pl.semaphore_signal(barrier, inc=1, device_id=device, device_id_type=MESH)

    greet(after)
    greet(before)

    def greet_xy(d):
        xx, yy = xy_to(d)
        greet(at(xx, yy, z, core))

    loop(1, XY, greet_xy)
    loop(1, Z, lambda d: greet(at(x, y, rem(z + d, Z), core)))
    greet(partner)

    row = lax.broadcasted_iota(jnp.int32, (M, 128), 0)
    col = lax.broadcasted_iota(jnp.int32, (M, 128), 1)

    def fill(t):
        size = sizes[first + t]
        for b in range(4):
            ok = (row < size) & (col < size - 128 * b)
            block = wave[t, :, 128 * b : 128 * b + 128].astype(F32)
            psi[0, t, b // 2, pl.ds(b % 2 * M, M), :] = jnp.where(ok, block, 0.0).astype(BF16)

    loop(0, 4, fill)
    for h in range(2):
        right_t[h] = right[0, 256 * h : 256 * h + 256, :].T
    own = [z * G + g if t == LAST else g * Z + z for t in range(4)]
    for t in range(4):
        chunk[t] = psi[0, t, core, rows(own[t], CHUNK), :].astype(F32)

    def columns(ref):
        return jnp.concatenate([ref[b // 2, pl.ds(b % 2 * M, M), :] for b in range(4)], axis=1)

    def compute(it, s):
        inner = jnp.dot(left[0], columns(psi.at[it, s]), preferred_element_type=F32).astype(BF16)
        theirs = jnp.dot(inner, right_t[1 - core], preferred_element_type=F32).astype(BF16)
        give[s, pl.ds(0, M), :] = theirs[:, :128]
        give[s, pl.ds(M, M), :] = theirs[:, 128:]
        mine = jnp.dot(inner, right_t[core], preferred_element_type=F32)
        acc[s, pl.ds(0, M), :] = mine[:, :128]
        acc[s, pl.ds(M, M), :] = mine[:, 128:]

    def source(a, t):
        s = rem(a * 4 + t - first - shift[0] + 2 * S, S)
        return jnp.minimum(s, 3), jnp.where(s < 4, 1.0, 0.0).astype(F32)

    def core_copy(it, t):
        return copy(csend.at[it, t], cland.at[it, t], c_s.at[it, t], c_r.at[it, t], partner)

    def pick(it, t):
        for a in range(2):
            s, gate = source(a, t)
            for b in range(4):
                part = pl.ds(256 * b, 256)
                csend[it, t, a, part, :] = (give[s, part, :].astype(F32) * gate).astype(BF16)

    def scatter(it, t):
        core_copy(it, t).wait_recv()
        for a in range(2):
            s, gate = source(a, t)
            for b in range(4):
                part = pl.ds(256 * b, 256)
                s1[it, t, a, part, :] = (
                    acc[s, part, :] * gate + cland[it, t, a, part, :].astype(F32)
                ).astype(BF16)
        sems = s1_s.at[it, t], s1_r.at[it, t]
        if t == LAST:

            def make(d):
                zz = rem(z + d, Z)
                return copy(s1.at[it, t, :, rows(zz, BLOCK)], l1z.at[it, d], *sems, at(x, y, zz, core))

            group(1, Z, make, l1z.at[it, pl.ds(1, Z - 1)], *sems)
        else:

            def make(d):
                xx, yy = xy_to(d)
                src = s1.at[it, t, rem(yy, 2), rows(div(yy, 2) * X + xx, BLOCK)]
                return copy(src, l1.at[it, t, d], *sems, at(xx, yy, z, core))

            group(1, XY, make, l1.at[it, t, pl.ds(1, XY - 1)], *sems)

    def reduce_first(it, t):
        sems = s1_s.at[it, t], s1_r.at[it, t]
        send = s2_s.at[it, t], s2_r.at[it, t]
        if t == LAST:
            arrived(l1z.at[it, pl.ds(1, Z - 1)], *sems)
            for a in range(2):
                value = s1[it, t, a, rows(z, BLOCK), :].astype(F32)
                for d in range(1, Z):
                    value = value + l1z[it, d, a].astype(F32)
                s2z[it, a] = value.astype(BF16)

            def make(d):
                xx, yy = xy_to(d)
                src = s2z.at[it, rem(yy, 2), rows(div(yy, 2) * X + xx, CHUNK)]
                return copy(src, l2z.at[it, d], *send, at(xx, yy, z, core))

            group(1, XY, make, l2z.at[it, pl.ds(1, XY - 1)], *send)
        else:
            arrived(l1.at[it, t, pl.ds(1, XY - 1)], *sems)
            value = s1[it, t, sec, rows(g, BLOCK), :].astype(F32)
            for d in range(1, XY):
                value = value + l1[it, t, d].astype(F32)
            s2[it, t] = value.astype(BF16)

            def make(d):
                zz = rem(z + d, Z)
                return copy(s2.at[it, t, rows(zz, CHUNK)], l2.at[it, t, d], *send, at(x, y, zz, core))

            group(1, Z, make, l2.at[it, t, pl.ds(1, Z - 1)], *send)

    def z_copies(ref, sems):
        return lambda d: copy(ref, ref, *sems, at(x, y, rem(z + d, Z), core))

    def g_copies(ref, sems):
        def make(d):
            xx, yy = g_to(d)
            return copy(ref, ref, *sems, at(xx, yy, z, core))

        return make

    def reduce_second(it, t):
        sems = s2_s.at[it, t], s2_r.at[it, t]
        if t == LAST:
            arrived(l2z.at[it, pl.ds(1, XY - 1)], *sems)
            value = s2z[it, sec, rows(g, CHUNK), :].astype(F32)
            for d in range(1, XY):
                value = value + l2z[it, d].astype(F32)
        else:
            arrived(l2.at[it, t, pl.ds(1, Z - 1)], *sems)
            value = s2[it, t, rows(z, CHUNK), :].astype(F32)
            for d in range(1, Z):
                value = value + l2[it, t, d].astype(F32)
        size = sizes[first + t]
        begin = own[t] * CHUNK
        r = lax.broadcasted_iota(jnp.int32, (CHUNK, 128), 0) + rem(begin, M)
        q = lax.broadcasted_iota(jnp.int32, (CHUNK, 128), 1) + (2 * core + div(begin, M)) * 128
        factor = steps[it].astype(F32) * (1.0 / (8.0 * math.sqrt(OPERATORS)))
        value = jnp.where((r < size) & (q < size), chunk[t] - factor * value, 0.0)
        chunk[t] = value
        psi[it + 1, t, core, rows(own[t], CHUNK), :] = value.astype(BF16)
        ref = psi.at[it + 1, t, core, rows(own[t], CHUNK)]
        send = a_s.at[it, t], a_r.at[it, t]
        whole = psi.at[it + 1, t, core, pl.ds(0, 7 * CHUNK)]
        group(1, 8, (g_copies if t == LAST else z_copies)(ref, send), whole, *send)

    def gather_second(it, t):
        arrived(psi.at[it + 1, t, core, pl.ds(0, 7 * CHUNK)], a_s.at[it, t], a_r.at[it, t])
        ref = psi.at[it + 1, t, core, rows(z if t == LAST else g, BLOCK)]
        send = b_s.at[it, t], b_r.at[it, t]
        if it == 1 and t == 0:
            src = psi.at[2, 0, core, rows(g, BLOCK)]
            dst = bas.at[core, rows(g, BLOCK)]

            def make(d):
                xx, yy = xy_to(rem(d, X) + X * (2 * div(d, X) + 1))
                return copy(src, dst, bas_s.at[0], bas_r.at[0], at(xx, yy, z, core))

            @pl.when(sec == 0)
            def _():
                loop(0, G, lambda d: make(d).start())

            @sent.append
            def _():
                @pl.when(sec == 0)
                def _():
                    copy(bas.at[0], bas.at[0], bas_s.at[0], bas_r.at[0], partner).wait_send()

        whole = psi.at[it + 1, t, core, pl.ds(0, 7 * BLOCK)]
        group(1, 8, (z_copies if t == LAST else g_copies)(ref, send), whole, *send)

    def forward_copy(it, t):
        ref = psi.at[it + 1, t, core]
        return copy(ref, ref, f_s.at[it, t], f_r.at[it, t], partner)

    def forward(it, t):
        arrived(psi.at[it + 1, t, core, pl.ds(0, 7 * BLOCK)], b_s.at[it, t], b_r.at[it, t])
        start(forward_copy(it, t))

    def norm_z(it):
        value = jnp.zeros((8, 128), F32)
        for t in range(4):
            part = chunk[t]
            value = value + jnp.sum((part * part).reshape(CHUNK // 8, 8, 128), axis=0)
        nz[it, 0] = value
        sems = n_s.at[it, 0], n_r.at[it, 0]

        def make(d):
            return copy(nz.at[it, 0], nz.at[it, d], *sems, at(x, y, rem(z + d, Z), core))

        group(1, Z, make, nz.at[it, pl.ds(1, Z - 1)], *sems)

    def norm_xy(it):
        arrived(nz.at[it, pl.ds(1, Z - 1)], n_s.at[it, 0], n_r.at[it, 0])
        nxy[it, 0] = jnp.sum(nz[it], axis=0)
        sems = n_s.at[it, 1], n_r.at[it, 1]

        def make(d):
            xx, yy = xy_to(d)
            return copy(nxy.at[it, 0], nxy.at[it, d], *sems, at(xx, yy, z, core))

        group(1, XY, make, nxy.at[it, pl.ds(1, XY - 1)], *sems)

    def norm_copy(it):
        return copy(nc.at[it, 0], nc.at[it, 1], n_s.at[it, 2], n_r.at[it, 2], partner)

    def norm_core(it):
        arrived(nxy.at[it, pl.ds(1, XY - 1)], n_s.at[it, 1], n_r.at[it, 1])
        nc[it, 0] = jnp.sum(nxy[it], axis=0)
        start(norm_copy(it))

    def norm_end(it):
        norm_copy(it).wait_recv()
        total[it] = nc[it, 0] + nc[it, 1]

    near_copies = [
        copy(left.at[0], near.at[0], near_s.at[0], near_r.at[0], after),
        copy(left.at[0], near.at[1], near_s.at[1], near_r.at[1], before),
    ]

    def mix():
        for c in near_copies:
            c.wait_recv()
        w0 = jnp.where(ops == 0, 0.0, integ[0, 0])
        w1 = integ[0, 1]
        w2 = jnp.where(ops == OPERATORS - 1, 0.0, integ[0, 2])

        def body(i):
            part = rows(i, 64)
            lmix[part, :] = (
                w0 * near[0, part, :].astype(F32)
                + w1 * left[0, part, :].astype(F32)
                + w2 * near[1, part, :].astype(F32)
            ).astype(BF16)

        loop(0, M // 64, body)

    def write_wave(t):
        for b in range(4):
            psi_out[t, :, 128 * b : 128 * b + 128] = psi[2, t, b // 2, pl.ds(b % 2 * M, M), :]

    bas_copy = copy(bas.at[core], bas.at[core], bas_s.at[1], bas_r.at[1], partner)

    def basis_forward():
        @pl.when(sec == 1)
        def _():
            arrived(bas.at[core], bas_s.at[0], bas_r.at[0])
            bas_copy.start()

        @sent.append
        def _():
            @pl.when(sec == 1)
            def _():
                bas_copy.wait_send()

    def rotate():
        @pl.when(sec == 0)
        def _():
            bas[...] = psi[2, 0]

        @pl.when(sec == 1)
        def _():
            bas_copy.wait_recv()

        basis_cols = jnp.concatenate([bas[sec, pl.ds(b * M, M), :] for b in range(2)], axis=1)
        half = jnp.dot(lmix[...], basis_cols, preferred_element_type=F32).astype(BF16)
        rotated[...] = lax.dot_general(
            columns(bas), half, (((0,), (0,)), ((), ())), preferred_element_type=F32
        )

    for s in range(4):
        compute(0, s)
    for it in range(2):
        for t in ORDER:
            pick(it, t)
            if it == 0 and t == ORDER[0]:
                pl.semaphore_wait(barrier, 3 + XY - 1 + Z - 1)
            start(core_copy(it, t))
        for t in ORDER:
            scatter(it, t)
            if it == 0 and t == LAST:
                for c in near_copies:
                    start(c)
        if it == 1:
            mix()
        reduce_first(it, 0)
        reduce_first(it, 3)
        reduce_first(it, 1)
        reduce_second(it, 0)
        reduce_first(it, 2)
        reduce_second(it, 3)
        reduce_second(it, 1)
        gather_second(it, 0)
        reduce_second(it, 2)
        norm_z(it)
        gather_second(it, 1)
        gather_second(it, 3)
        forward(it, 0)
        if it == 1:
            basis_forward()
        gather_second(it, 2)
        norm_xy(it)
        forward(it, 1)
        forward(it, 3)
        forward_copy(it, 0).wait_recv()
        if it == 0:
            compute(1, 0)
        else:
            write_wave(0)
            rotate()
        forward_copy(it, 1).wait_recv()
        if it == 0:
            compute(1, 1)
        else:
            write_wave(1)
        forward(it, 2)
        norm_core(it)
        for t in (3, 2):
            forward_copy(it, t).wait_recv()
            if it == 0:
                compute(1, t)
            else:
                write_wave(t)
        norm_end(it)

    count = float(S * M * M)
    sum1 = jnp.sum(total[0], axis=(0, 1), keepdims=True)
    sum2 = jnp.sum(total[1], axis=(0, 1), keepdims=True)
    square = sum2 * (1.0 / count) + 1e-06 * (sum1 * (1.0 / count) + 1e-06)
    scale = lax.rsqrt(square)
    scale_out[...] = jnp.broadcast_to(scale, (1, M))
    mixed_out[0] = (rotated[...] * (scale * scale * (1.0 / M))).astype(BF16)

    for wait in sent:
        wait()


def shards(*args):
    vmem = pl.BlockSpec(memory_space=pltpu.VMEM)
    smem = pl.BlockSpec(memory_space=pltpu.SMEM)

    def low(*shape):
        return pltpu.VMEM(shape, BF16)

    def full(*shape):
        return pltpu.VMEM(shape, F32)

    def pair(*shape):
        return [pltpu.SemaphoreType.DMA(shape)] * 2

    wave, mixed, scale = pl.pallas_call(
        kernel,
        out_shape=(
            jax.ShapeDtypeStruct((4, M, M), BF16),
            jax.ShapeDtypeStruct((1, M, M // 2), BF16),
            jax.ShapeDtypeStruct((1, M), F32),
        ),
        in_specs=[vmem, vmem, vmem, smem, smem, smem, smem],
        out_specs=(vmem, vmem, vmem),
        scratch_shapes=[
            low(3, 4, 2, HALF, 128),
            low(2, HALF, 128),
            low(2, M, 256),
            low(2, M, M),
            low(M, M),
            full(4, CHUNK, 128),
            low(4, HALF, 128),
            full(4, HALF, 128),
            low(2, 4, 2, HALF, 128),
            low(2, 4, 2, HALF, 128),
            low(2, 4, 2, HALF, 128),
            low(2, 3, XY, BLOCK, 128),
            low(2, Z, 2, BLOCK, 128),
            low(2, 3, BLOCK, 128),
            low(2, 2, BLOCK, 128),
            low(2, 3, Z, CHUNK, 128),
            low(2, XY, CHUNK, 128),
            full(2, Z, 8, 128),
            full(2, XY, 8, 128),
            full(2, 2, 8, 128),
            full(2, 8, 128),
            full(M, M // 2),
            *pair(2),
            *pair(2, 4),
            *pair(2, 4),
            *pair(2, 4),
            *pair(2, 4),
            *pair(2, 4),
            *pair(2, 4),
            *pair(2),
            *pair(2, 3),
        ],
        compiler_params=pltpu.CompilerParams(
            collective_id=0, has_side_effects=True, vmem_limit_bytes=60 * 2**20
        ),
        name="dmrg_window",
    )(*args)
    return wave.astype(F32) * scale, mixed


def solution(mesh):
    placed = (
        P("sec", None, None),
        P("ops", None, None),
        P("ops", None, None),
        P("ops"),
        P(),
        P(),
        P("ops", None),
    )
    return jax.shard_map(
        shards,
        mesh=mesh,
        in_specs=placed,
        out_specs=(P("sec", None, None), P("ops", None, "sec")),
        check_vma=False,
    )
```

```python
import math

import jax
import jax.numpy as jnp
from jax import lax
from jax.experimental import pallas as pl
from jax.experimental.pallas import tpu as pltpu
from jax.sharding import PartitionSpec as P

MESH = pl.DeviceIdType.MESH
F32 = jnp.float32
BF16 = jnp.bfloat16
M = 512
S = 8
OPERATORS = 128
YH, X, Z = 2, 4, 8
G = YH * X
Y = 2 * YH
XY = X * Y
HALF = 2 * M
CHUNK = HALF // (G * Z)
BLOCK = HALF // 8
LAST = 3
ORDER = (3, 0, 1, 2)


def loop(low, high, body):
    lax.fori_loop(low, high, lambda i, c: (body(i), c)[1], 0)


def rem(a, b):
    return lax.rem(a, jnp.int32(b))


def div(a, b):
    return lax.div(a, jnp.int32(b))


def rows(o, n):
    return pl.ds(pl.multiple_of(o * n, n), n)


def kernel(
    wave, left, right, shift, sizes, steps, integ,
    psi_out, mixed_out, scale_out,
    psi, bas, right_t, near, lmix, chunk, acc,
    shifts, csend, cland, s1, l1, l1z, s2, s2z, l2, l2z, nz, nxy, nc, total, rotated,
    near_s, near_r, c_s, c_r, s1_s, s1_r, s2_s, s2_r, a_s, a_r, b_s, b_r, f_s, f_r, bas_s, bas_r, n_s, n_r, sh_s, sh_r,
):
    ops = lax.axis_index("ops")
    sec = lax.axis_index("sec")
    core = rem(ops, 2)
    z = rem(div(ops, 2), Z)
    x = rem(div(ops, 2 * Z), X)
    yh = div(ops, 2 * Z * X)
    y = yh * 2 + sec
    g = yh * X + x
    first = sec * 4

    def at(xx, yy, zz, cc):
        return ((div(yy, 2) * X + xx) * Z + zz) * 2 + cc, rem(yy, 2)

    def xy_to(d):
        return rem(x + rem(d, X), X), rem(y + div(d, X), Y)

    def g_to(d):
        return rem(x + rem(d, X), X), rem(y + 2 * div(d, X), Y)

    partner = at(x, y, z, 1 - core)
    after = (rem(ops + 1, OPERATORS), sec)
    before = (rem(ops + OPERATORS - 1, OPERATORS), sec)

    def copy(src, dst, send, recv, device):
        return pltpu.make_async_remote_copy(
            src_ref=src, dst_ref=dst, send_sem=send, recv_sem=recv, device_id=device, device_id_type=MESH
        )

    sent = []

    def start(made):
        made.start()
        sent.append(made.wait_send)

    def group(low, high, make, whole, send, recv):
        loop(low, high, lambda d: make(d).start())
        sent.append(copy(whole, whole, send, recv, partner).wait_send)

    def arrived(whole, send, recv):
        copy(whole, whole, send, recv, partner).wait_recv()

    barrier = pltpu.get_barrier_semaphore()

    def greet(device):
        pl.semaphore_signal(barrier, inc=1, device_id=device, device_id_type=MESH)

    greet(after)
    greet(before)

    def greet_xy(d):
        xx, yy = xy_to(d)
        greet(at(xx, yy, z, core))

    loop(1, XY, greet_xy)
    loop(1, Z, lambda d: greet(at(x, y, rem(z + d, Z), core)))
    greet(partner)

    row = lax.broadcasted_iota(jnp.int32, (M, 128), 0)
    col = lax.broadcasted_iota(jnp.int32, (M, 128), 1)

    def fill(t):
        size = sizes[first + t]
        for b in range(4):
            ok = (row < size) & (col < size - 128 * b)
            block = wave[t, :, 128 * b : 128 * b + 128].astype(F32)
            psi[0, t, b // 2, pl.ds(b % 2 * M, M), :] = jnp.where(ok, block, 0.0).astype(BF16)

    shifts[0, 0] = shift[0]
    loop(0, 4, fill)
    for h in range(2):
        right_t[h] = right[0, 256 * h : 256 * h + 256, :].T
    own = [z * G + g if t == LAST else g * Z + z for t in range(4)]
    for t in range(4):
        chunk[t] = psi[0, t, core, rows(own[t], CHUNK), :].astype(F32)

    def columns(ref):
        return jnp.concatenate([ref[b // 2, pl.ds(b % 2 * M, M), :] for b in range(4)], axis=1)

    def compute(it, s):
        inner = jnp.dot(left[0], columns(psi.at[it, s]), preferred_element_type=F32).astype(BF16)
        theirs = jnp.dot(inner, right_t[1 - core], preferred_element_type=F32).astype(BF16)
        csend[it, s, pl.ds(0, M), :] = theirs[:, :128]
        csend[it, s, pl.ds(M, M), :] = theirs[:, 128:]
        if it or s > 1:
            exchange(it, s)
        mine = jnp.dot(inner, right_t[core], preferred_element_type=F32)
        acc[s, pl.ds(0, M), :] = mine[:, :128]
        acc[s, pl.ds(M, M), :] = mine[:, 128:]

    def source(a, t, by):
        s = rem(a * 4 + t - first - by + 2 * S, S)
        return jnp.minimum(s, 3), jnp.where(s < 4, 1.0, 0.0).astype(F32)

    def core_copy(it, t):
        return copy(csend.at[it, t], cland.at[it, t], c_s.at[it, t], c_r.at[it, t], partner)

    def exchange(it, s):
        start(core_copy(it, s))

    def scatter(it, t):
        for a in range(2):
            s, gate = source(a, t, shift[0])
            ps, pgate = source(a, t, shifts[1, 0])
            for b in range(4):
                part = pl.ds(256 * b, 256)
                s1[it, t, a, part, :] = (
                    acc[s, part, :] * gate + cland[it, ps, part, :].astype(F32) * pgate
                ).astype(BF16)
        sems = s1_s.at[it, t], s1_r.at[it, t]
        if t == LAST:

            def make(d):
                zz = rem(z + d, Z)
                return copy(s1.at[it, t, :, rows(zz, BLOCK)], l1z.at[it, d], *sems, at(x, y, zz, core))

            group(1, Z, make, l1z.at[it, pl.ds(1, Z - 1)], *sems)
        else:

            def make(d):
                xx, yy = xy_to(d)
                src = s1.at[it, t, rem(yy, 2), rows(div(yy, 2) * X + xx, BLOCK)]
                return copy(src, l1.at[it, t, d], *sems, at(xx, yy, z, core))

            group(1, XY, make, l1.at[it, t, pl.ds(1, XY - 1)], *sems)

    def reduce_first(it, t):
        sems = s1_s.at[it, t], s1_r.at[it, t]
        send = s2_s.at[it, t], s2_r.at[it, t]
        if t == LAST:
            arrived(l1z.at[it, pl.ds(1, Z - 1)], *sems)
            for a in range(2):
                value = s1[it, t, a, rows(z, BLOCK), :].astype(F32)
                for d in range(1, Z):
                    value = value + l1z[it, d, a].astype(F32)
                s2z[it, a] = value.astype(BF16)

            def make(d):
                xx, yy = xy_to(d)
                src = s2z.at[it, rem(yy, 2), rows(div(yy, 2) * X + xx, CHUNK)]
                return copy(src, l2z.at[it, d], *send, at(xx, yy, z, core))

            group(1, XY, make, l2z.at[it, pl.ds(1, XY - 1)], *send)
        else:
            arrived(l1.at[it, t, pl.ds(1, XY - 1)], *sems)
            value = s1[it, t, sec, rows(g, BLOCK), :].astype(F32)
            for d in range(1, XY):
                value = value + l1[it, t, d].astype(F32)
            s2[it, t] = value.astype(BF16)

            def make(d):
                zz = rem(z + d, Z)
                return copy(s2.at[it, t, rows(zz, CHUNK)], l2.at[it, t, d], *send, at(x, y, zz, core))

            group(1, Z, make, l2.at[it, t, pl.ds(1, Z - 1)], *send)

    def z_copies(ref, sems):
        return lambda d: copy(ref, ref, *sems, at(x, y, rem(z + d, Z), core))

    def g_copies(ref, sems):
        def make(d):
            xx, yy = g_to(d)
            return copy(ref, ref, *sems, at(xx, yy, z, core))

        return make

    def reduce_second(it, t):
        sems = s2_s.at[it, t], s2_r.at[it, t]
        if t == LAST:
            arrived(l2z.at[it, pl.ds(1, XY - 1)], *sems)
            value = s2z[it, sec, rows(g, CHUNK), :].astype(F32)
            for d in range(1, XY):
                value = value + l2z[it, d].astype(F32)
        else:
            arrived(l2.at[it, t, pl.ds(1, Z - 1)], *sems)
            value = s2[it, t, rows(z, CHUNK), :].astype(F32)
            for d in range(1, Z):
                value = value + l2[it, t, d].astype(F32)
        size = sizes[first + t]
        begin = own[t] * CHUNK
        r = lax.broadcasted_iota(jnp.int32, (CHUNK, 128), 0) + rem(begin, M)
        q = lax.broadcasted_iota(jnp.int32, (CHUNK, 128), 1) + (2 * core + div(begin, M)) * 128
        factor = steps[it].astype(F32) * (1.0 / (8.0 * math.sqrt(OPERATORS)))
        value = jnp.where((r < size) & (q < size), chunk[t] - factor * value, 0.0)
        chunk[t] = value
        psi[it + 1, t, core, rows(own[t], CHUNK), :] = value.astype(BF16)
        ref = psi.at[it + 1, t, core, rows(own[t], CHUNK)]
        send = a_s.at[it, t], a_r.at[it, t]
        whole = psi.at[it + 1, t, core, pl.ds(0, 7 * CHUNK)]
        group(1, 8, (g_copies if t == LAST else z_copies)(ref, send), whole, *send)

    def gather_second(it, t):
        arrived(psi.at[it + 1, t, core, pl.ds(0, 7 * CHUNK)], a_s.at[it, t], a_r.at[it, t])
        ref = psi.at[it + 1, t, core, rows(z if t == LAST else g, BLOCK)]
        send = b_s.at[it, t], b_r.at[it, t]
        if it == 1 and t == 0:
            src = psi.at[2, 0, core, rows(g, BLOCK)]
            dst = bas.at[core, rows(g, BLOCK)]

            def make(d):
                xx, yy = xy_to(rem(d, X) + X * (2 * div(d, X) + 1))
                return copy(src, dst, bas_s.at[0], bas_r.at[0], at(xx, yy, z, core))

            @pl.when(sec == 0)
            def _():
                loop(0, G, lambda d: make(d).start())

            @sent.append
            def _():
                @pl.when(sec == 0)
                def _():
                    copy(bas.at[0], bas.at[0], bas_s.at[0], bas_r.at[0], partner).wait_send()

        whole = psi.at[it + 1, t, core, pl.ds(0, 7 * BLOCK)]
        group(1, 8, (z_copies if t == LAST else g_copies)(ref, send), whole, *send)

    def forward_copy(it, t):
        ref = psi.at[it + 1, t, core]
        return copy(ref, ref, f_s.at[it, t], f_r.at[it, t], partner)

    def forward(it, t):
        arrived(psi.at[it + 1, t, core, pl.ds(0, 7 * BLOCK)], b_s.at[it, t], b_r.at[it, t])
        start(forward_copy(it, t))

    def norm_z(it):
        value = jnp.zeros((8, 128), F32)
        for t in range(4):
            part = chunk[t]
            value = value + jnp.sum((part * part).reshape(CHUNK // 8, 8, 128), axis=0)
        nz[it, 0] = value
        sems = n_s.at[it, 0], n_r.at[it, 0]

        def make(d):
            return copy(nz.at[it, 0], nz.at[it, d], *sems, at(x, y, rem(z + d, Z), core))

        group(1, Z, make, nz.at[it, pl.ds(1, Z - 1)], *sems)

    def norm_xy(it):
        arrived(nz.at[it, pl.ds(1, Z - 1)], n_s.at[it, 0], n_r.at[it, 0])
        nxy[it, 0] = jnp.sum(nz[it], axis=0)
        sems = n_s.at[it, 1], n_r.at[it, 1]

        def make(d):
            xx, yy = xy_to(d)
            return copy(nxy.at[it, 0], nxy.at[it, d], *sems, at(xx, yy, z, core))

        group(1, XY, make, nxy.at[it, pl.ds(1, XY - 1)], *sems)

    def norm_copy(it):
        return copy(nc.at[it, 0], nc.at[it, 1], n_s.at[it, 2], n_r.at[it, 2], partner)

    def norm_core(it):
        arrived(nxy.at[it, pl.ds(1, XY - 1)], n_s.at[it, 1], n_r.at[it, 1])
        nc[it, 0] = jnp.sum(nxy[it], axis=0)
        start(norm_copy(it))

    def norm_end(it):
        norm_copy(it).wait_recv()
        total[it] = nc[it, 0] + nc[it, 1]

    near_copies = [
        copy(left.at[0], near.at[0], near_s.at[0], near_r.at[0], after),
        copy(left.at[0], near.at[1], near_s.at[1], near_r.at[1], before),
    ]

    def mix():
        for c in near_copies:
            c.wait_recv()
        w0 = jnp.where(ops == 0, 0.0, integ[0, 0])
        w1 = integ[0, 1]
        w2 = jnp.where(ops == OPERATORS - 1, 0.0, integ[0, 2])

        def body(i):
            part = rows(i, 64)
            lmix[part, :] = (
                w0 * near[0, part, :].astype(F32)
                + w1 * left[0, part, :].astype(F32)
                + w2 * near[1, part, :].astype(F32)
            ).astype(BF16)

        loop(0, M // 64, body)

    def write_wave(t):
        for b in range(4):
            psi_out[t, :, 128 * b : 128 * b + 128] = psi[2, t, b // 2, pl.ds(b % 2 * M, M), :]

    bas_copy = copy(bas.at[core], bas.at[core], bas_s.at[1], bas_r.at[1], partner)

    def basis_forward():
        @pl.when(sec == 1)
        def _():
            arrived(bas.at[core], bas_s.at[0], bas_r.at[0])
            bas_copy.start()

        @sent.append
        def _():
            @pl.when(sec == 1)
            def _():
                bas_copy.wait_send()

    def rotate():
        @pl.when(sec == 0)
        def _():
            bas[...] = psi[2, 0]

        @pl.when(sec == 1)
        def _():
            bas_copy.wait_recv()

        basis_cols = jnp.concatenate([bas[sec, pl.ds(b * M, M), :] for b in range(2)], axis=1)
        half = jnp.dot(lmix[...], basis_cols, preferred_element_type=F32).astype(BF16)
        rotated[...] = lax.dot_general(
            columns(bas), half, (((0,), (0,)), ((), ())), preferred_element_type=F32
        )

    shift_copy = copy(shifts.at[0], shifts.at[1], sh_s.at[0], sh_r.at[0], partner)
    for s in range(4):
        compute(0, s)
        if s == 1:
            pl.semaphore_wait(barrier, 3 + XY - 1 + Z - 1)
            start(shift_copy)
            exchange(0, 0)
            exchange(0, 1)
    shift_copy.wait_recv()
    for it in range(2):
        for s in (0, 1, 3, 2):
            core_copy(it, s).wait_recv()
        for t in ORDER:
            scatter(it, t)
        if it == 1:
            mix()
        reduce_first(it, 0)
        reduce_first(it, 3)
        if it == 0:
            for c in near_copies:
                start(c)
        reduce_first(it, 1)
        reduce_second(it, 0)
        reduce_first(it, 2)
        reduce_second(it, 3)
        reduce_second(it, 1)
        gather_second(it, 0)
        reduce_second(it, 2)
        norm_z(it)
        gather_second(it, 1)
        gather_second(it, 3)
        forward(it, 0)
        if it == 1:
            basis_forward()
        gather_second(it, 2)
        norm_xy(it)
        forward(it, 1)
        forward(it, 3)
        forward_copy(it, 0).wait_recv()
        if it == 0:
            compute(1, 0)
        else:
            write_wave(0)
            rotate()
        forward_copy(it, 1).wait_recv()
        if it == 0:
            compute(1, 1)
        else:
            write_wave(1)
        forward(it, 2)
        norm_core(it)
        for t in (3, 2):
            forward_copy(it, t).wait_recv()
            if it == 0:
                compute(1, t)
            else:
                write_wave(t)
        norm_end(it)

    count = float(S * M * M)
    sum1 = jnp.sum(total[0], axis=(0, 1), keepdims=True)
    sum2 = jnp.sum(total[1], axis=(0, 1), keepdims=True)
    square = sum2 * (1.0 / count) + 1e-06 * (sum1 * (1.0 / count) + 1e-06)
    scale = lax.rsqrt(square)
    scale_out[...] = jnp.broadcast_to(scale, (1, M))
    mixed_out[0] = (rotated[...] * (scale * scale * (1.0 / M))).astype(BF16)

    for wait in sent:
        wait()


def finish(wave, mixed, scale, wave_out, mixed_out):
    wave_out[...] = wave[...].astype(F32) * scale[...]
    mixed_out[...] = mixed[...]


def shards(*args):
    vmem = pl.BlockSpec(memory_space=pltpu.VMEM)
    smem = pl.BlockSpec(memory_space=pltpu.SMEM)

    def low(*shape):
        return pltpu.VMEM(shape, BF16)

    def full(*shape):
        return pltpu.VMEM(shape, F32)

    def pair(*shape):
        return [pltpu.SemaphoreType.DMA(shape)] * 2

    wave, mixed, scale = pl.pallas_call(
        kernel,
        out_shape=(
            jax.ShapeDtypeStruct((4, M, M), BF16),
            jax.ShapeDtypeStruct((1, M, M // 2), BF16),
            jax.ShapeDtypeStruct((1, M), F32),
        ),
        in_specs=[vmem, vmem, vmem, smem, smem, smem, smem],
        out_specs=(vmem, vmem, vmem),
        scratch_shapes=[
            low(3, 4, 2, HALF, 128),
            low(2, HALF, 128),
            low(2, M, 256),
            low(2, M, M),
            low(M, M),
            full(4, CHUNK, 128),
            full(4, HALF, 128),
            pltpu.SMEM((2, 1), jnp.int32),
            low(2, 4, HALF, 128),
            low(2, 4, HALF, 128),
            low(2, 4, 2, HALF, 128),
            low(2, 3, XY, BLOCK, 128),
            low(2, Z, 2, BLOCK, 128),
            low(2, 3, BLOCK, 128),
            low(2, 2, BLOCK, 128),
            low(2, 3, Z, CHUNK, 128),
            low(2, XY, CHUNK, 128),
            full(2, Z, 8, 128),
            full(2, XY, 8, 128),
            full(2, 2, 8, 128),
            full(2, 8, 128),
            full(M, M // 2),
            *pair(2),
            *pair(2, 4),
            *pair(2, 4),
            *pair(2, 4),
            *pair(2, 4),
            *pair(2, 4),
            *pair(2, 4),
            *pair(2),
            *pair(2, 3),
            *pair(1),
        ],
        compiler_params=pltpu.CompilerParams(
            collective_id=0, has_side_effects=True, vmem_limit_bytes=60 * 2**20
        ),
        name="dmrg_window",
    )(*args)
    steps = 8
    return pl.pallas_call(
        finish,
        grid=(steps,),
        out_shape=(
            jax.ShapeDtypeStruct((4, M, M), F32),
            jax.ShapeDtypeStruct((1, M, M // 2), BF16),
        ),
        in_specs=[
            pl.BlockSpec((1, M // 2, M), lambda i: (i // 2, i % 2, 0)),
            pl.BlockSpec((1, M // steps, M // 2), lambda i: (0, i, 0)),
            pl.BlockSpec((1, M), lambda i: (0, 0)),
        ],
        out_specs=(
            pl.BlockSpec((1, M // 2, M), lambda i: (i // 2, i % 2, 0)),
            pl.BlockSpec((1, M // steps, M // 2), lambda i: (0, i, 0)),
        ),
        name="scale_wave",
    )(wave, mixed, scale)


def solution(mesh):
    placed = (
        P("sec", None, None),
        P("ops", None, None),
        P("ops", None, None),
        P("ops"),
        P(),
        P(),
        P("ops", None),
    )
    return jax.shard_map(
        shards,
        mesh=mesh,
        in_specs=placed,
        out_specs=(P("sec", None, None), P("ops", None, "sec")),
        check_vma=False,
    )
```

```python
import math

import jax
import jax.numpy as jnp
from jax import lax
from jax.experimental import pallas as pl
from jax.experimental.pallas import tpu as pltpu
from jax.sharding import PartitionSpec as P

MESH = pl.DeviceIdType.MESH
F32 = jnp.float32
BF16 = jnp.bfloat16
M = 512
S = 8
OPERATORS = 128
YH, X, Z = 2, 4, 8
G = YH * X
Y = 2 * YH
XY = X * Y
HALF = 2 * M
CHUNK = HALF // (G * Z)
BLOCK = HALF // 8
LAST = 3
ORDER = (3, 0, 1, 2)


def loop(low, high, body):
    lax.fori_loop(low, high, lambda i, c: (body(i), c)[1], 0)


def rem(a, b):
    return lax.rem(a, jnp.int32(b))


def div(a, b):
    return lax.div(a, jnp.int32(b))


def rows(o, n):
    return pl.ds(pl.multiple_of(o * n, n), n)


def kernel(
    wave_hbm, left_hbm, right_hbm, shift_hbm, sizes, steps, integ,
    psi_out, mixed_out, scale_out,
    wave, left, right, shift, psi, bas, right_t, near, lmix, chunk, acc,
    shifts, csend, cland, s1, l1, l1z, s2, s2z, l2, l2z, nz, nxy, nc, total, rotated,
    near_s, near_r, c_s, c_r, s1_s, s1_r, s2_s, s2_r, a_s, a_r, b_s, b_r, f_s, f_r, bas_s, bas_r, n_s, n_r, sh_s, sh_r, in_s,
):
    ops = lax.axis_index("ops")
    sec = lax.axis_index("sec")
    core = rem(ops, 2)
    z = rem(div(ops, 2), Z)
    x = rem(div(ops, 2 * Z), X)
    yh = div(ops, 2 * Z * X)
    y = yh * 2 + sec
    g = yh * X + x
    first = sec * 4

    def at(xx, yy, zz, cc):
        return ((div(yy, 2) * X + xx) * Z + zz) * 2 + cc, rem(yy, 2)

    def xy_to(d):
        return rem(x + rem(d, X), X), rem(y + div(d, X), Y)

    def g_to(d):
        return rem(x + rem(d, X), X), rem(y + 2 * div(d, X), Y)

    partner = at(x, y, z, 1 - core)
    after = (rem(ops + 1, OPERATORS), sec)
    before = (rem(ops + OPERATORS - 1, OPERATORS), sec)

    def copy(src, dst, send, recv, device):
        return pltpu.make_async_remote_copy(
            src_ref=src, dst_ref=dst, send_sem=send, recv_sem=recv, device_id=device, device_id_type=MESH
        )

    sent = []

    def start(made):
        made.start()
        sent.append(made.wait_send)

    def group(low, high, make, whole, send, recv):
        if high - low < 8:
            for d in range(low, high):
                make(jnp.int32(d)).start()
        else:
            loop(low, high, lambda d: make(d).start())
        sent.append(copy(whole, whole, send, recv, partner).wait_send)

    def arrived(whole, send, recv):
        copy(whole, whole, send, recv, partner).wait_recv()

    inputs = [pltpu.make_async_copy(wave_hbm.at[t], wave.at[t], in_s.at[t]) for t in range(4)]
    inputs.append(pltpu.make_async_copy(left_hbm, left, in_s.at[4]))
    inputs.append(pltpu.make_async_copy(right_hbm, right, in_s.at[5]))
    inputs.append(pltpu.make_async_copy(shift_hbm, shift, in_s.at[6]))
    for t in (6, 0, 5, 4, 1, 2, 3):
        inputs[t].start()

    barrier = pltpu.get_barrier_semaphore()

    def greet(device):
        pl.semaphore_signal(barrier, inc=1, device_id=device, device_id_type=MESH)

    greet(after)
    greet(before)

    def greet_xy(d):
        xx, yy = xy_to(d)
        greet(at(xx, yy, z, core))

    loop(1, XY, greet_xy)
    loop(1, Z, lambda d: greet(at(x, y, rem(z + d, Z), core)))
    greet(partner)

    row = lax.broadcasted_iota(jnp.int32, (M, 128), 0)
    col = lax.broadcasted_iota(jnp.int32, (M, 128), 1)

    def fill(t):
        size = sizes[first + t]
        for b in range(4):
            ok = (row < size) & (col < size - 128 * b)
            block = wave[t, :, 128 * b : 128 * b + 128].astype(F32)
            psi[0, t, b // 2, pl.ds(b % 2 * M, M), :] = jnp.where(ok, block, 0.0).astype(BF16)

    inputs[6].wait()
    shifts[0, 0] = shift[0]
    for t in range(4):
        inputs[t].wait()
        fill(t)
    inputs[5].wait()
    for h in range(2):
        right_t[h] = right[0, 256 * h : 256 * h + 256, :].T
    own = [z * G + g if t == LAST else g * Z + z for t in range(4)]
    for t in range(4):
        chunk[t] = psi[0, t, core, rows(own[t], CHUNK), :].astype(F32)

    inputs[4].wait()

    def columns(ref):
        return jnp.concatenate([ref[b // 2, pl.ds(b % 2 * M, M), :] for b in range(4)], axis=1)

    def compute(it, s):
        inner = jnp.dot(left[0], columns(psi.at[it, s]), preferred_element_type=F32).astype(BF16)
        theirs = jnp.dot(inner, right_t[1 - core], preferred_element_type=F32).astype(BF16)
        csend[it, s, pl.ds(0, M), :] = theirs[:, :128]
        csend[it, s, pl.ds(M, M), :] = theirs[:, 128:]
        if it or s > 1:
            exchange(it, s)
        mine = jnp.dot(inner, right_t[core], preferred_element_type=F32)
        acc[s, pl.ds(0, M), :] = mine[:, :128]
        acc[s, pl.ds(M, M), :] = mine[:, 128:]

    def source(a, t, by):
        s = rem(a * 4 + t - first - by + 2 * S, S)
        return jnp.minimum(s, 3), jnp.where(s < 4, 1.0, 0.0).astype(F32)

    def core_copy(it, t):
        return copy(csend.at[it, t], cland.at[it, t], c_s.at[it, t], c_r.at[it, t], partner)

    def exchange(it, s):
        start(core_copy(it, s))

    def scatter(it, t):
        for a in range(2):
            s, gate = source(a, t, shift[0])
            ps, pgate = source(a, t, shifts[1, 0])
            for b in range(4):
                part = pl.ds(256 * b, 256)
                s1[it, t, a, part, :] = (
                    acc[s, part, :] * gate + cland[it, ps, part, :].astype(F32) * pgate
                ).astype(BF16)
        sems = s1_s.at[it, t], s1_r.at[it, t]
        if t == LAST:

            def make(d):
                zz = rem(z + d, Z)
                return copy(s1.at[it, t, :, rows(zz, BLOCK)], l1z.at[it, d], *sems, at(x, y, zz, core))

            group(1, Z, make, l1z.at[it, pl.ds(1, Z - 1)], *sems)
        else:

            def make(d):
                xx, yy = xy_to(d)
                src = s1.at[it, t, rem(yy, 2), rows(div(yy, 2) * X + xx, BLOCK)]
                return copy(src, l1.at[it, t, d], *sems, at(xx, yy, z, core))

            group(1, XY, make, l1.at[it, t, pl.ds(1, XY - 1)], *sems)

    def reduce_first(it, t):
        sems = s1_s.at[it, t], s1_r.at[it, t]
        send = s2_s.at[it, t], s2_r.at[it, t]
        if t == LAST:
            arrived(l1z.at[it, pl.ds(1, Z - 1)], *sems)
            for a in range(2):
                value = s1[it, t, a, rows(z, BLOCK), :].astype(F32)
                for d in range(1, Z):
                    value = value + l1z[it, d, a].astype(F32)
                s2z[it, a] = value.astype(BF16)

            def make(d):
                xx, yy = xy_to(d)
                src = s2z.at[it, rem(yy, 2), rows(div(yy, 2) * X + xx, CHUNK)]
                return copy(src, l2z.at[it, d], *send, at(xx, yy, z, core))

            group(1, XY, make, l2z.at[it, pl.ds(1, XY - 1)], *send)
        else:
            arrived(l1.at[it, t, pl.ds(1, XY - 1)], *sems)
            value = s1[it, t, sec, rows(g, BLOCK), :].astype(F32)
            for d in range(1, XY):
                value = value + l1[it, t, d].astype(F32)
            s2[it, t] = value.astype(BF16)

            def make(d):
                zz = rem(z + d, Z)
                return copy(s2.at[it, t, rows(zz, CHUNK)], l2.at[it, t, d], *send, at(x, y, zz, core))

            group(1, Z, make, l2.at[it, t, pl.ds(1, Z - 1)], *send)

    def z_copies(ref, sems):
        return lambda d: copy(ref, ref, *sems, at(x, y, rem(z + d, Z), core))

    def g_copies(ref, sems):
        def make(d):
            xx, yy = g_to(d)
            return copy(ref, ref, *sems, at(xx, yy, z, core))

        return make

    def reduce_second(it, t):
        sems = s2_s.at[it, t], s2_r.at[it, t]
        if t == LAST:
            arrived(l2z.at[it, pl.ds(1, XY - 1)], *sems)
            value = s2z[it, sec, rows(g, CHUNK), :].astype(F32)
            for d in range(1, XY):
                value = value + l2z[it, d].astype(F32)
        else:
            arrived(l2.at[it, t, pl.ds(1, Z - 1)], *sems)
            value = s2[it, t, rows(z, CHUNK), :].astype(F32)
            for d in range(1, Z):
                value = value + l2[it, t, d].astype(F32)
        size = sizes[first + t]
        begin = own[t] * CHUNK
        r = lax.broadcasted_iota(jnp.int32, (CHUNK, 128), 0) + rem(begin, M)
        q = lax.broadcasted_iota(jnp.int32, (CHUNK, 128), 1) + (2 * core + div(begin, M)) * 128
        factor = steps[it].astype(F32) * (1.0 / (8.0 * math.sqrt(OPERATORS)))
        value = jnp.where((r < size) & (q < size), chunk[t] - factor * value, 0.0)
        chunk[t] = value
        psi[it + 1, t, core, rows(own[t], CHUNK), :] = value.astype(BF16)
        ref = psi.at[it + 1, t, core, rows(own[t], CHUNK)]
        send = a_s.at[it, t], a_r.at[it, t]
        whole = psi.at[it + 1, t, core, pl.ds(0, 7 * CHUNK)]
        group(1, 8, (g_copies if t == LAST else z_copies)(ref, send), whole, *send)

    def gather_second(it, t):
        arrived(psi.at[it + 1, t, core, pl.ds(0, 7 * CHUNK)], a_s.at[it, t], a_r.at[it, t])
        ref = psi.at[it + 1, t, core, rows(z if t == LAST else g, BLOCK)]
        send = b_s.at[it, t], b_r.at[it, t]
        if it == 1 and t == 0:
            src = psi.at[2, 0, core, rows(g, BLOCK)]
            dst = bas.at[core, rows(g, BLOCK)]

            def make(d):
                xx, yy = xy_to(rem(d, X) + X * (2 * div(d, X) + 1))
                return copy(src, dst, bas_s.at[0], bas_r.at[0], at(xx, yy, z, core))

            @pl.when(sec == 0)
            def _():
                loop(0, G, lambda d: make(d).start())

            @sent.append
            def _():
                @pl.when(sec == 0)
                def _():
                    copy(bas.at[0], bas.at[0], bas_s.at[0], bas_r.at[0], partner).wait_send()

        whole = psi.at[it + 1, t, core, pl.ds(0, 7 * BLOCK)]
        group(1, 8, (z_copies if t == LAST else g_copies)(ref, send), whole, *send)

    def forward_copy(it, t):
        ref = psi.at[it + 1, t, core]
        return copy(ref, ref, f_s.at[it, t], f_r.at[it, t], partner)

    def forward(it, t):
        arrived(psi.at[it + 1, t, core, pl.ds(0, 7 * BLOCK)], b_s.at[it, t], b_r.at[it, t])
        start(forward_copy(it, t))

    def norm_z(it):
        value = jnp.zeros((8, 128), F32)
        for t in range(4):
            part = chunk[t]
            value = value + jnp.sum((part * part).reshape(CHUNK // 8, 8, 128), axis=0)
        nz[it, 0] = value
        sems = n_s.at[it, 0], n_r.at[it, 0]

        def make(d):
            return copy(nz.at[it, 0], nz.at[it, d], *sems, at(x, y, rem(z + d, Z), core))

        group(1, Z, make, nz.at[it, pl.ds(1, Z - 1)], *sems)

    def norm_xy(it):
        arrived(nz.at[it, pl.ds(1, Z - 1)], n_s.at[it, 0], n_r.at[it, 0])
        nxy[it, 0] = jnp.sum(nz[it], axis=0)
        sems = n_s.at[it, 1], n_r.at[it, 1]

        def make(d):
            xx, yy = xy_to(d)
            return copy(nxy.at[it, 0], nxy.at[it, d], *sems, at(xx, yy, z, core))

        group(1, XY, make, nxy.at[it, pl.ds(1, XY - 1)], *sems)

    def norm_copy(it):
        return copy(nc.at[it, 0], nc.at[it, 1], n_s.at[it, 2], n_r.at[it, 2], partner)

    def norm_core(it):
        arrived(nxy.at[it, pl.ds(1, XY - 1)], n_s.at[it, 1], n_r.at[it, 1])
        nc[it, 0] = jnp.sum(nxy[it], axis=0)
        start(norm_copy(it))

    def norm_end(it):
        norm_copy(it).wait_recv()
        total[it] = nc[it, 0] + nc[it, 1]

    near_copies = [
        copy(left.at[0], near.at[0], near_s.at[0], near_r.at[0], after),
        copy(left.at[0], near.at[1], near_s.at[1], near_r.at[1], before),
    ]

    def mix():
        for c in near_copies:
            c.wait_recv()
        w0 = jnp.where(ops == 0, 0.0, integ[0, 0])
        w1 = integ[0, 1]
        w2 = jnp.where(ops == OPERATORS - 1, 0.0, integ[0, 2])

        def body(i):
            part = rows(i, 64)
            lmix[part, :] = (
                w0 * near[0, part, :].astype(F32)
                + w1 * left[0, part, :].astype(F32)
                + w2 * near[1, part, :].astype(F32)
            ).astype(BF16)

        loop(0, M // 64, body)

    def write_wave(t):
        for b in range(4):
            psi_out[t, :, 128 * b : 128 * b + 128] = psi[2, t, b // 2, pl.ds(b % 2 * M, M), :]

    bas_copy = copy(bas.at[core], bas.at[core], bas_s.at[1], bas_r.at[1], partner)

    def basis_forward():
        @pl.when(sec == 1)
        def _():
            arrived(bas.at[core], bas_s.at[0], bas_r.at[0])
            bas_copy.start()

        @sent.append
        def _():
            @pl.when(sec == 1)
            def _():
                bas_copy.wait_send()

    def rotate():
        @pl.when(sec == 0)
        def _():
            bas[...] = psi[2, 0]

        @pl.when(sec == 1)
        def _():
            bas_copy.wait_recv()

        basis_cols = jnp.concatenate([bas[sec, pl.ds(b * M, M), :] for b in range(2)], axis=1)
        half = jnp.dot(lmix[...], basis_cols, preferred_element_type=F32).astype(BF16)
        rotated[...] = lax.dot_general(
            columns(bas), half, (((0,), (0,)), ((), ())), preferred_element_type=F32
        )

    shift_copy = copy(shifts.at[0], shifts.at[1], sh_s.at[0], sh_r.at[0], partner)
    for s in range(4):
        compute(0, s)
        if s == 1:
            pl.semaphore_wait(barrier, 3 + XY - 1 + Z - 1)
            start(shift_copy)
            exchange(0, 0)
            exchange(0, 1)
    shift_copy.wait_recv()
    for it in range(2):
        for s in (0, 1, 3, 2):
            core_copy(it, s).wait_recv()
        for t in ORDER:
            scatter(it, t)
            if it == 1 and t == LAST:
                for c in near_copies:
                    start(c)
        reduce_first(it, 0)
        reduce_first(it, 3)
        reduce_first(it, 1)
        reduce_second(it, 0)
        reduce_first(it, 2)
        reduce_second(it, 3)
        reduce_second(it, 1)
        gather_second(it, 0)
        reduce_second(it, 2)
        norm_z(it)
        if it == 1:
            mix()
        gather_second(it, 1)
        gather_second(it, 3)
        forward(it, 0)
        if it == 1:
            basis_forward()
        gather_second(it, 2)
        norm_xy(it)
        forward(it, 1)
        forward(it, 3)
        forward_copy(it, 0).wait_recv()
        if it == 0:
            compute(1, 0)
        else:
            write_wave(0)
            rotate()
        forward_copy(it, 1).wait_recv()
        if it == 0:
            compute(1, 1)
        else:
            write_wave(1)
        forward(it, 2)
        norm_core(it)
        for t in (3, 2):
            forward_copy(it, t).wait_recv()
            if it == 0:
                compute(1, t)
            else:
                write_wave(t)
        norm_end(it)

    count = float(S * M * M)
    sum1 = jnp.sum(total[0], axis=(0, 1), keepdims=True)
    sum2 = jnp.sum(total[1], axis=(0, 1), keepdims=True)
    square = sum2 * (1.0 / count) + 1e-06 * (sum1 * (1.0 / count) + 1e-06)
    scale = lax.rsqrt(square)
    scale_out[...] = jnp.broadcast_to(scale, (1, M))
    mixed_out[0] = (rotated[...] * (scale * scale * (1.0 / M))).astype(BF16)

    for wait in sent:
        wait()


def shards(*args):
    vmem = pl.BlockSpec(memory_space=pltpu.VMEM)
    smem = pl.BlockSpec(memory_space=pltpu.SMEM)
    hbm = pl.BlockSpec(memory_space=pltpu.HBM)

    def low(*shape):
        return pltpu.VMEM(shape, BF16)

    def full(*shape):
        return pltpu.VMEM(shape, F32)

    def pair(*shape):
        return [pltpu.SemaphoreType.DMA(shape)] * 2

    wave, mixed, scale = pl.pallas_call(
        kernel,
        out_shape=(
            jax.ShapeDtypeStruct((4, M, M), BF16),
            jax.ShapeDtypeStruct((1, M, M // 2), BF16),
            jax.ShapeDtypeStruct((1, M), F32),
        ),
        in_specs=[hbm, hbm, hbm, hbm, smem, smem, smem],
        out_specs=(vmem, vmem, vmem),
        scratch_shapes=[
            low(4, M, M),
            low(1, M, M),
            low(1, M, M),
            pltpu.SMEM((1,), jnp.int32),
            low(3, 4, 2, HALF, 128),
            low(2, HALF, 128),
            low(2, M, 256),
            low(2, M, M),
            low(M, M),
            full(4, CHUNK, 128),
            full(4, HALF, 128),
            pltpu.SMEM((2, 1), jnp.int32),
            low(2, 4, HALF, 128),
            low(2, 4, HALF, 128),
            low(2, 4, 2, HALF, 128),
            low(2, 3, XY, BLOCK, 128),
            low(2, Z, 2, BLOCK, 128),
            low(2, 3, BLOCK, 128),
            low(2, 2, BLOCK, 128),
            low(2, 3, Z, CHUNK, 128),
            low(2, XY, CHUNK, 128),
            full(2, Z, 8, 128),
            full(2, XY, 8, 128),
            full(2, 2, 8, 128),
            full(2, 8, 128),
            full(M, M // 2),
            *pair(2),
            *pair(2, 4),
            *pair(2, 4),
            *pair(2, 4),
            *pair(2, 4),
            *pair(2, 4),
            *pair(2, 4),
            *pair(2),
            *pair(2, 3),
            *pair(1),
            pltpu.SemaphoreType.DMA((7,)),
        ],
        compiler_params=pltpu.CompilerParams(
            collective_id=0, has_side_effects=True, vmem_limit_bytes=60 * 2**20
        ),
        name="dmrg_window",
    )(*args)
    return wave.astype(F32) * scale, mixed


def solution(mesh):
    placed = (
        P("sec", None, None),
        P("ops", None, None),
        P("ops", None, None),
        P("ops"),
        P(),
        P(),
        P("ops", None),
    )
    return jax.shard_map(
        shards,
        mesh=mesh,
        in_specs=placed,
        out_specs=(P("sec", None, None), P("ops", None, "sec")),
        check_vma=False,
    )
```

```python
import math

import jax
import jax.numpy as jnp
from jax import lax
from jax.experimental import pallas as pl
from jax.experimental.pallas import tpu as pltpu
from jax.sharding import PartitionSpec as P

MESH = pl.DeviceIdType.MESH
F32 = jnp.float32
BF16 = jnp.bfloat16
M = 512
S = 8
OPERATORS = 128
YH, X, Z = 2, 4, 8
G = YH * X
Y = 2 * YH
XY = X * Y
HALF = 2 * M
CHUNK = HALF // (G * Z)
BLOCK = HALF // 8
LAST = 3
ORDER = (0, 3, 1, 2)


def loop(low, high, body):
    lax.fori_loop(low, high, lambda i, c: (body(i), c)[1], 0)


def rem(a, b):
    return lax.rem(a, jnp.int32(b))


def div(a, b):
    return lax.div(a, jnp.int32(b))


def rows(o, n):
    return pl.ds(pl.multiple_of(o * n, n), n)


def kernel(
    wave_hbm, left_hbm, right_hbm, shift_hbm, sizes, steps, integ,
    psi_out, mixed_out, scale_out,
    wave, left, right, shift, psi, bas, right_t, near, lmix, chunk, acc,
    shifts, csend, cland, s1, l1, l1z, s2, s2z, l2, l2z, nz, nxy, nc, total, rotated,
    near_s, near_r, c_s, c_r, s1_s, s1_r, s2_s, s2_r, a_s, a_r, b_s, b_r, f_s, f_r, bas_s, bas_r, n_s, n_r, sh_s, sh_r, in_s,
):
    ops = lax.axis_index("ops")
    sec = lax.axis_index("sec")
    core = rem(ops, 2)
    z = rem(div(ops, 2), Z)
    x = rem(div(ops, 2 * Z), X)
    yh = div(ops, 2 * Z * X)
    y = yh * 2 + sec
    g = yh * X + x
    first = sec * 4

    def at(xx, yy, zz, cc):
        return ((div(yy, 2) * X + xx) * Z + zz) * 2 + cc, rem(yy, 2)

    def xy_to(d):
        return rem(x + rem(d, X), X), rem(y + div(d, X), Y)

    def g_to(d):
        return rem(x + rem(d, X), X), rem(y + 2 * div(d, X), Y)

    partner = at(x, y, z, 1 - core)
    after = (rem(ops + 1, OPERATORS), sec)
    before = (rem(ops + OPERATORS - 1, OPERATORS), sec)

    def copy(src, dst, send, recv, device):
        return pltpu.make_async_remote_copy(
            src_ref=src, dst_ref=dst, send_sem=send, recv_sem=recv, device_id=device, device_id_type=MESH
        )

    sent = []

    def start(made):
        made.start()
        sent.append(made.wait_send)

    def group(low, high, make, whole, send, recv):
        if high - low < 8:
            for d in range(low, high):
                make(jnp.int32(d)).start()
        else:
            loop(low, high, lambda d: make(d).start())
        sent.append(copy(whole, whole, send, recv, partner).wait_send)

    def arrived(whole, send, recv):
        copy(whole, whole, send, recv, partner).wait_recv()

    inputs = [pltpu.make_async_copy(wave_hbm.at[t], wave.at[t], in_s.at[t]) for t in range(4)]
    inputs.append(pltpu.make_async_copy(left_hbm, left, in_s.at[4]))
    inputs.append(pltpu.make_async_copy(right_hbm, right, in_s.at[5]))
    inputs.append(pltpu.make_async_copy(shift_hbm, shift, in_s.at[6]))
    for t in (6, 0, 5, 4, 1, 2, 3):
        inputs[t].start()

    barrier = pltpu.get_barrier_semaphore()

    def greet(device):
        pl.semaphore_signal(barrier, inc=1, device_id=device, device_id_type=MESH)

    greet(after)
    greet(before)

    def greet_xy(d):
        xx, yy = xy_to(d)
        greet(at(xx, yy, z, core))

    loop(1, XY, greet_xy)
    loop(1, Z, lambda d: greet(at(x, y, rem(z + d, Z), core)))
    greet(partner)

    row = lax.broadcasted_iota(jnp.int32, (M, 128), 0)
    col = lax.broadcasted_iota(jnp.int32, (M, 128), 1)

    def fill(t):
        size = sizes[first + t]
        for b in range(4):
            ok = (row < size) & (col < size - 128 * b)
            block = wave[t, :, 128 * b : 128 * b + 128].astype(F32)
            psi[0, t, b // 2, pl.ds(b % 2 * M, M), :] = jnp.where(ok, block, 0.0).astype(BF16)

    inputs[6].wait()
    shifts[0, 0] = shift[0]
    for t in range(4):
        inputs[t].wait()
        fill(t)
    inputs[5].wait()
    for h in range(2):
        right_t[h] = right[0, 256 * h : 256 * h + 256, :].T
    own = [z * G + g if t == LAST else g * Z + z for t in range(4)]
    for t in range(4):
        chunk[t] = psi[0, t, core, rows(own[t], CHUNK), :].astype(F32)

    inputs[4].wait()

    def columns(ref):
        return jnp.concatenate([ref[b // 2, pl.ds(b % 2 * M, M), :] for b in range(4)], axis=1)

    def compute(it, s):
        inner = jnp.dot(left[0], columns(psi.at[it, s]), preferred_element_type=F32).astype(BF16)
        theirs = jnp.dot(inner, right_t[1 - core], preferred_element_type=F32).astype(BF16)
        csend[it, s, pl.ds(0, M), :] = theirs[:, :128]
        csend[it, s, pl.ds(M, M), :] = theirs[:, 128:]
        if it or s > 1:
            exchange(it, s)
        mine = jnp.dot(inner, right_t[core], preferred_element_type=F32)
        acc[s, pl.ds(0, M), :] = mine[:, :128]
        acc[s, pl.ds(M, M), :] = mine[:, 128:]

    def source(a, t, by):
        s = rem(a * 4 + t - first - by + 2 * S, S)
        return jnp.minimum(s, 3), jnp.where(s < 4, 1.0, 0.0).astype(F32)

    def core_copy(it, t):
        return copy(csend.at[it, t], cland.at[it, t], c_s.at[it, t], c_r.at[it, t], partner)

    def exchange(it, s):
        start(core_copy(it, s))

    def scatter(it, t):
        for a in range(2):
            s, gate = source(a, t, shift[0])
            ps, pgate = source(a, t, shifts[1, 0])
            for b in range(4):
                part = pl.ds(256 * b, 256)
                s1[it, t, a, part, :] = (
                    acc[s, part, :] * gate + cland[it, ps, part, :].astype(F32) * pgate
                ).astype(BF16)
        sems = s1_s.at[it, t], s1_r.at[it, t]
        if t == LAST:

            def make(d):
                zz = rem(z + d, Z)
                return copy(s1.at[it, t, :, rows(zz, BLOCK)], l1z.at[it, d], *sems, at(x, y, zz, core))

            group(1, Z, make, l1z.at[it, pl.ds(1, Z - 1)], *sems)
        else:

            def make(d):
                xx, yy = xy_to(d)
                src = s1.at[it, t, rem(yy, 2), rows(div(yy, 2) * X + xx, BLOCK)]
                return copy(src, l1.at[it, t, d], *sems, at(xx, yy, z, core))

            group(1, XY, make, l1.at[it, t, pl.ds(1, XY - 1)], *sems)

    def reduce_first(it, t):
        sems = s1_s.at[it, t], s1_r.at[it, t]
        send = s2_s.at[it, t], s2_r.at[it, t]
        if t == LAST:
            arrived(l1z.at[it, pl.ds(1, Z - 1)], *sems)
            for a in range(2):
                value = s1[it, t, a, rows(z, BLOCK), :].astype(F32)
                for d in range(1, Z):
                    value = value + l1z[it, d, a].astype(F32)
                s2z[it, a] = value.astype(BF16)

            def make(d):
                xx, yy = xy_to(d)
                src = s2z.at[it, rem(yy, 2), rows(div(yy, 2) * X + xx, CHUNK)]
                return copy(src, l2z.at[it, d], *send, at(xx, yy, z, core))

            group(1, XY, make, l2z.at[it, pl.ds(1, XY - 1)], *send)
        else:
            arrived(l1.at[it, t, pl.ds(1, XY - 1)], *sems)
            value = s1[it, t, sec, rows(g, BLOCK), :].astype(F32)
            for d in range(1, XY):
                value = value + l1[it, t, d].astype(F32)
            s2[it, t] = value.astype(BF16)

            def make(d):
                zz = rem(z + d, Z)
                return copy(s2.at[it, t, rows(zz, CHUNK)], l2.at[it, t, d], *send, at(x, y, zz, core))

            group(1, Z, make, l2.at[it, t, pl.ds(1, Z - 1)], *send)

    def z_copies(ref, sems):
        return lambda d: copy(ref, ref, *sems, at(x, y, rem(z + d, Z), core))

    def g_copies(ref, sems):
        def make(d):
            xx, yy = g_to(d)
            return copy(ref, ref, *sems, at(xx, yy, z, core))

        return make

    def reduce_second(it, t):
        sems = s2_s.at[it, t], s2_r.at[it, t]
        if t == LAST:
            arrived(l2z.at[it, pl.ds(1, XY - 1)], *sems)
            value = s2z[it, sec, rows(g, CHUNK), :].astype(F32)
            for d in range(1, XY):
                value = value + l2z[it, d].astype(F32)
        else:
            arrived(l2.at[it, t, pl.ds(1, Z - 1)], *sems)
            value = s2[it, t, rows(z, CHUNK), :].astype(F32)
            for d in range(1, Z):
                value = value + l2[it, t, d].astype(F32)
        size = sizes[first + t]
        begin = own[t] * CHUNK
        r = lax.broadcasted_iota(jnp.int32, (CHUNK, 128), 0) + rem(begin, M)
        q = lax.broadcasted_iota(jnp.int32, (CHUNK, 128), 1) + (2 * core + div(begin, M)) * 128
        factor = steps[it].astype(F32) * (1.0 / (8.0 * math.sqrt(OPERATORS)))
        value = jnp.where((r < size) & (q < size), chunk[t] - factor * value, 0.0)
        chunk[t] = value
        psi[it + 1, t, core, rows(own[t], CHUNK), :] = value.astype(BF16)
        ref = psi.at[it + 1, t, core, rows(own[t], CHUNK)]
        send = a_s.at[it, t], a_r.at[it, t]
        whole = psi.at[it + 1, t, core, pl.ds(0, 7 * CHUNK)]
        group(1, 8, (g_copies if t == LAST else z_copies)(ref, send), whole, *send)

    def gather_second(it, t):
        arrived(psi.at[it + 1, t, core, pl.ds(0, 7 * CHUNK)], a_s.at[it, t], a_r.at[it, t])
        ref = psi.at[it + 1, t, core, rows(z if t == LAST else g, BLOCK)]
        send = b_s.at[it, t], b_r.at[it, t]
        if it == 1 and t == 0:
            src = psi.at[2, 0, core, rows(g, BLOCK)]
            dst = bas.at[core, rows(g, BLOCK)]

            def make(d):
                xx, yy = xy_to(rem(d, X) + X * (2 * div(d, X) + 1))
                return copy(src, dst, bas_s.at[0], bas_r.at[0], at(xx, yy, z, core))

            @pl.when(sec == 0)
            def _():
                loop(0, G, lambda d: make(d).start())

            @sent.append
            def _():
                @pl.when(sec == 0)
                def _():
                    copy(bas.at[0], bas.at[0], bas_s.at[0], bas_r.at[0], partner).wait_send()

        whole = psi.at[it + 1, t, core, pl.ds(0, 7 * BLOCK)]
        group(1, 8, (z_copies if t == LAST else g_copies)(ref, send), whole, *send)

    def forward_copy(it, t):
        ref = psi.at[it + 1, t, core]
        return copy(ref, ref, f_s.at[it, t], f_r.at[it, t], partner)

    def forward(it, t):
        arrived(psi.at[it + 1, t, core, pl.ds(0, 7 * BLOCK)], b_s.at[it, t], b_r.at[it, t])
        start(forward_copy(it, t))

    def norm_z(it):
        value = jnp.zeros((8, 128), F32)
        for t in range(4):
            part = chunk[t]
            value = value + jnp.sum((part * part).reshape(CHUNK // 8, 8, 128), axis=0)
        nz[it, 0] = value
        sems = n_s.at[it, 0], n_r.at[it, 0]

        def make(d):
            return copy(nz.at[it, 0], nz.at[it, d], *sems, at(x, y, rem(z + d, Z), core))

        group(1, Z, make, nz.at[it, pl.ds(1, Z - 1)], *sems)

    def norm_xy(it):
        arrived(nz.at[it, pl.ds(1, Z - 1)], n_s.at[it, 0], n_r.at[it, 0])
        nxy[it, 0] = jnp.sum(nz[it], axis=0)
        sems = n_s.at[it, 1], n_r.at[it, 1]

        def make(d):
            xx, yy = xy_to(d)
            return copy(nxy.at[it, 0], nxy.at[it, d], *sems, at(xx, yy, z, core))

        group(1, XY, make, nxy.at[it, pl.ds(1, XY - 1)], *sems)

    def norm_copy(it):
        return copy(nc.at[it, 0], nc.at[it, 1], n_s.at[it, 2], n_r.at[it, 2], partner)

    def norm_core(it):
        arrived(nxy.at[it, pl.ds(1, XY - 1)], n_s.at[it, 1], n_r.at[it, 1])
        nc[it, 0] = jnp.sum(nxy[it], axis=0)
        start(norm_copy(it))

    def norm_end(it):
        norm_copy(it).wait_recv()
        total[it] = nc[it, 0] + nc[it, 1]

    near_copies = [
        copy(left.at[0], near.at[0], near_s.at[0], near_r.at[0], after),
        copy(left.at[0], near.at[1], near_s.at[1], near_r.at[1], before),
    ]

    def mix():
        for c in near_copies:
            c.wait_recv()
        w0 = jnp.where(ops == 0, 0.0, integ[0, 0])
        w1 = integ[0, 1]
        w2 = jnp.where(ops == OPERATORS - 1, 0.0, integ[0, 2])

        def body(i):
            part = rows(i, 64)
            lmix[part, :] = (
                w0 * near[0, part, :].astype(F32)
                + w1 * left[0, part, :].astype(F32)
                + w2 * near[1, part, :].astype(F32)
            ).astype(BF16)

        loop(0, M // 64, body)

    def write_wave(t):
        for b in range(4):
            psi_out[t, :, 128 * b : 128 * b + 128] = psi[2, t, b // 2, pl.ds(b % 2 * M, M), :]

    bas_copy = copy(bas.at[core], bas.at[core], bas_s.at[1], bas_r.at[1], partner)

    def basis_forward():
        @pl.when(sec == 1)
        def _():
            arrived(bas.at[core], bas_s.at[0], bas_r.at[0])
            bas_copy.start()

        @sent.append
        def _():
            @pl.when(sec == 1)
            def _():
                bas_copy.wait_send()

    def rotate():
        @pl.when(sec == 0)
        def _():
            bas[...] = psi[2, 0]

        @pl.when(sec == 1)
        def _():
            bas_copy.wait_recv()

        basis_cols = jnp.concatenate([bas[sec, pl.ds(b * M, M), :] for b in range(2)], axis=1)
        half = jnp.dot(lmix[...], basis_cols, preferred_element_type=F32).astype(BF16)
        rotated[...] = lax.dot_general(
            columns(bas), half, (((0,), (0,)), ((), ())), preferred_element_type=F32
        )

    shift_copy = copy(shifts.at[0], shifts.at[1], sh_s.at[0], sh_r.at[0], partner)
    for s in range(4):
        compute(0, s)
        if s == 1:
            pl.semaphore_wait(barrier, 3 + XY - 1 + Z - 1)
            start(shift_copy)
            exchange(0, 0)
            exchange(0, 1)
    shift_copy.wait_recv()
    for it in range(2):
        for s in (0, 1, 3, 2):
            core_copy(it, s).wait_recv()
        for t in ORDER:
            scatter(it, t)
            if it == 1 and t == LAST:
                for c in near_copies:
                    start(c)
        if it == 1:
            norm_z(0)
        reduce_first(it, 0)
        reduce_first(it, 3)
        reduce_first(it, 1)
        if it == 1:
            norm_xy(0)
        reduce_second(it, 0)
        reduce_first(it, 2)
        reduce_second(it, 3)
        reduce_second(it, 1)
        gather_second(it, 0)
        reduce_second(it, 2)
        if it == 1:
            norm_z(1)
        gather_second(it, 1)
        gather_second(it, 3)
        if it == 1:
            norm_core(0)
            mix()
        forward(it, 0)
        if it == 1:
            basis_forward()
        if it == 1:
            norm_xy(1)
        gather_second(it, 2)
        forward(it, 1)
        forward_copy(it, 0).wait_recv()
        if it == 0:
            compute(1, 0)
        else:
            write_wave(0)
            rotate()
        forward_copy(it, 1).wait_recv()
        if it == 0:
            compute(1, 1)
        else:
            write_wave(1)
        forward(it, 3)
        forward(it, 2)
        if it == 1:
            norm_core(1)
        for t in (3, 2):
            forward_copy(it, t).wait_recv()
            if it == 0:
                compute(1, t)
            else:
                write_wave(t)
    norm_end(0)
    norm_end(1)

    count = float(S * M * M)
    sum1 = jnp.sum(total[0], axis=(0, 1), keepdims=True)
    sum2 = jnp.sum(total[1], axis=(0, 1), keepdims=True)
    square = sum2 * (1.0 / count) + 1e-06 * (sum1 * (1.0 / count) + 1e-06)
    scale = lax.rsqrt(square)
    scale_out[...] = jnp.broadcast_to(scale, (1, M))
    mixed_out[0] = (rotated[...] * (scale * scale * (1.0 / M))).astype(BF16)

    for wait in sent:
        wait()


def shards(*args):
    vmem = pl.BlockSpec(memory_space=pltpu.VMEM)
    smem = pl.BlockSpec(memory_space=pltpu.SMEM)
    hbm = pl.BlockSpec(memory_space=pltpu.HBM)

    def low(*shape):
        return pltpu.VMEM(shape, BF16)

    def full(*shape):
        return pltpu.VMEM(shape, F32)

    def pair(*shape):
        return [pltpu.SemaphoreType.DMA(shape)] * 2

    wave, mixed, scale = pl.pallas_call(
        kernel,
        out_shape=(
            jax.ShapeDtypeStruct((4, M, M), BF16),
            jax.ShapeDtypeStruct((1, M, M // 2), BF16),
            jax.ShapeDtypeStruct((1, M), F32),
        ),
        in_specs=[hbm, hbm, hbm, hbm, smem, smem, smem],
        out_specs=(vmem, vmem, vmem),
        scratch_shapes=[
            low(4, M, M),
            low(1, M, M),
            low(1, M, M),
            pltpu.SMEM((1,), jnp.int32),
            low(3, 4, 2, HALF, 128),
            low(2, HALF, 128),
            low(2, M, 256),
            low(2, M, M),
            low(M, M),
            full(4, CHUNK, 128),
            full(4, HALF, 128),
            pltpu.SMEM((2, 1), jnp.int32),
            low(2, 4, HALF, 128),
            low(2, 4, HALF, 128),
            low(2, 4, 2, HALF, 128),
            low(2, 3, XY, BLOCK, 128),
            low(2, Z, 2, BLOCK, 128),
            low(2, 3, BLOCK, 128),
            low(2, 2, BLOCK, 128),
            low(2, 3, Z, CHUNK, 128),
            low(2, XY, CHUNK, 128),
            full(2, Z, 8, 128),
            full(2, XY, 8, 128),
            full(2, 2, 8, 128),
            full(2, 8, 128),
            full(M, M // 2),
            *pair(2),
            *pair(2, 4),
            *pair(2, 4),
            *pair(2, 4),
            *pair(2, 4),
            *pair(2, 4),
            *pair(2, 4),
            *pair(2),
            *pair(2, 3),
            *pair(1),
            pltpu.SemaphoreType.DMA((7,)),
        ],
        compiler_params=pltpu.CompilerParams(
            collective_id=0, has_side_effects=True, vmem_limit_bytes=60 * 2**20
        ),
        name="dmrg_window",
    )(*args)
    return wave.astype(F32) * scale, mixed


def solution(mesh):
    placed = (
        P("sec", None, None),
        P("ops", None, None),
        P("ops", None, None),
        P("ops"),
        P(),
        P(),
        P("ops", None),
    )
    return jax.shard_map(
        shards,
        mesh=mesh,
        in_specs=placed,
        out_specs=(P("sec", None, None), P("ops", None, "sec")),
        check_vma=False,
    )
```

```python
import math

import jax
import jax.numpy as jnp
from jax import lax
from jax.experimental import pallas as pl
from jax.experimental.pallas import tpu as pltpu
from jax.sharding import PartitionSpec as P

MESH = pl.DeviceIdType.MESH
F32 = jnp.float32
BF16 = jnp.bfloat16
M = 512
S = 8
OPERATORS = 128
YH, X, Z = 2, 4, 8
G = YH * X
Y = 2 * YH
XY = X * Y
HALF = 2 * M
CHUNK = HALF // (G * Z)
BLOCK = HALF // 8
LAST = 3
ORDER = (0, 3, 1, 2)


def loop(low, high, body):
    lax.fori_loop(low, high, lambda i, c: (body(i), c)[1], 0)


def rem(a, b):
    return lax.rem(a, jnp.int32(b))


def div(a, b):
    return lax.div(a, jnp.int32(b))


def rows(o, n):
    return pl.ds(pl.multiple_of(o * n, n), n)


def kernel(
    wave_hbm, left_hbm, right_hbm, shift_hbm, sizes, steps, integ,
    psi_hbm, mixed_out, scale_out,
    wave, left, right, shift, psi_out, psi, bas, right_t, near, lmix, chunk, acc,
    shifts, csend, cland, s1, l1, l1z, s2, s2z, l2, l2z, nz, nxy, nc, total, rotated,
    near_s, near_r, c_s, c_r, s1_s, s1_r, s2_s, s2_r, a_s, a_r, b_s, b_r, f_s, f_r, bas_s, bas_r, n_s, n_r, sh_s, sh_r, in_s, out_s,
):
    ops = lax.axis_index("ops")
    sec = lax.axis_index("sec")
    core = rem(ops, 2)
    z = rem(div(ops, 2), Z)
    x = rem(div(ops, 2 * Z), X)
    yh = div(ops, 2 * Z * X)
    y = yh * 2 + sec
    g = yh * X + x
    first = sec * 4

    def at(xx, yy, zz, cc):
        return ((div(yy, 2) * X + xx) * Z + zz) * 2 + cc, rem(yy, 2)

    def xy_to(d):
        return rem(x + rem(d, X), X), rem(y + div(d, X), Y)

    def g_to(d):
        return rem(x + rem(d, X), X), rem(y + 2 * div(d, X), Y)

    partner = at(x, y, z, 1 - core)
    after = (rem(ops + 1, OPERATORS), sec)
    before = (rem(ops + OPERATORS - 1, OPERATORS), sec)

    def copy(src, dst, send, recv, device):
        return pltpu.make_async_remote_copy(
            src_ref=src, dst_ref=dst, send_sem=send, recv_sem=recv, device_id=device, device_id_type=MESH
        )

    sent = []

    def start(made):
        made.start()
        sent.append(made.wait_send)

    def group(low, high, make, whole, send, recv):
        if high - low < 8:
            for d in range(low, high):
                make(jnp.int32(d)).start()
        else:
            loop(low, high, lambda d: make(d).start())
        sent.append(copy(whole, whole, send, recv, partner).wait_send)

    def arrived(whole, send, recv):
        copy(whole, whole, send, recv, partner).wait_recv()

    inputs = [pltpu.make_async_copy(wave_hbm.at[t], wave.at[t], in_s.at[t]) for t in range(4)]
    inputs.append(pltpu.make_async_copy(left_hbm, left, in_s.at[4]))
    inputs.append(pltpu.make_async_copy(right_hbm, right, in_s.at[5]))
    inputs.append(pltpu.make_async_copy(shift_hbm, shift, in_s.at[6]))
    for t in (6, 0, 5, 4, 1, 2, 3):
        inputs[t].start()

    barrier = pltpu.get_barrier_semaphore()

    def greet(device):
        pl.semaphore_signal(barrier, inc=1, device_id=device, device_id_type=MESH)

    greet(after)
    greet(before)

    def greet_xy(d):
        xx, yy = xy_to(d)
        greet(at(xx, yy, z, core))

    loop(1, XY, greet_xy)
    loop(1, Z, lambda d: greet(at(x, y, rem(z + d, Z), core)))
    greet(partner)

    row = lax.broadcasted_iota(jnp.int32, (M, 128), 0)
    col = lax.broadcasted_iota(jnp.int32, (M, 128), 1)

    def fill(t):
        size = sizes[first + t]
        for b in range(4):
            ok = (row < size) & (col < size - 128 * b)
            block = wave[t, :, 128 * b : 128 * b + 128].astype(F32)
            psi[0, t, b // 2, pl.ds(b % 2 * M, M), :] = jnp.where(ok, block, 0.0).astype(BF16)

    inputs[6].wait()
    shifts[0, 0] = shift[0]
    for t in range(4):
        inputs[t].wait()
        fill(t)
    inputs[5].wait()
    for h in range(2):
        right_t[h] = right[0, 256 * h : 256 * h + 256, :].T
    own = [z * G + g if t == LAST else g * Z + z for t in range(4)]
    for t in range(4):
        chunk[t] = psi[0, t, core, rows(own[t], CHUNK), :].astype(F32)

    inputs[4].wait()

    def columns(ref):
        return jnp.concatenate([ref[b // 2, pl.ds(b % 2 * M, M), :] for b in range(4)], axis=1)

    def compute(it, s):
        inner = jnp.dot(left[0], columns(psi.at[it, s]), preferred_element_type=F32).astype(BF16)
        theirs = jnp.dot(inner, right_t[1 - core], preferred_element_type=F32).astype(BF16)
        csend[it, s, pl.ds(0, M), :] = theirs[:, :128]
        csend[it, s, pl.ds(M, M), :] = theirs[:, 128:]
        if it or s > 1:
            exchange(it, s)
        mine = jnp.dot(inner, right_t[core], preferred_element_type=F32)
        acc[s, pl.ds(0, M), :] = mine[:, :128]
        acc[s, pl.ds(M, M), :] = mine[:, 128:]

    def source(a, t, by):
        s = rem(a * 4 + t - first - by + 2 * S, S)
        return jnp.minimum(s, 3), jnp.where(s < 4, 1.0, 0.0).astype(F32)

    def core_copy(it, t):
        return copy(csend.at[it, t], cland.at[it, t], c_s.at[it, t], c_r.at[it, t], partner)

    def exchange(it, s):
        start(core_copy(it, s))

    def scatter(it, t):
        for a in range(2):
            s, gate = source(a, t, shift[0])
            ps, pgate = source(a, t, shifts[1, 0])
            for b in range(4):
                part = pl.ds(256 * b, 256)
                s1[it, t, a, part, :] = (
                    acc[s, part, :] * gate + cland[it, ps, part, :].astype(F32) * pgate
                ).astype(BF16)
        sems = s1_s.at[it, t], s1_r.at[it, t]
        if t == LAST:

            def make(d):
                zz = rem(z + d, Z)
                return copy(s1.at[it, t, :, rows(zz, BLOCK)], l1z.at[it, d], *sems, at(x, y, zz, core))

            group(1, Z, make, l1z.at[it, pl.ds(1, Z - 1)], *sems)
        else:

            def make(d):
                xx, yy = xy_to(d)
                src = s1.at[it, t, rem(yy, 2), rows(div(yy, 2) * X + xx, BLOCK)]
                return copy(src, l1.at[it, t, d], *sems, at(xx, yy, z, core))

            group(1, XY, make, l1.at[it, t, pl.ds(1, XY - 1)], *sems)

    def reduce_first(it, t):
        sems = s1_s.at[it, t], s1_r.at[it, t]
        send = s2_s.at[it, t], s2_r.at[it, t]
        if t == LAST:
            arrived(l1z.at[it, pl.ds(1, Z - 1)], *sems)
            for a in range(2):
                value = s1[it, t, a, rows(z, BLOCK), :].astype(F32)
                for d in range(1, Z):
                    value = value + l1z[it, d, a].astype(F32)
                s2z[it, a] = value.astype(BF16)

            def make(d):
                xx, yy = xy_to(d)
                src = s2z.at[it, rem(yy, 2), rows(div(yy, 2) * X + xx, CHUNK)]
                return copy(src, l2z.at[it, d], *send, at(xx, yy, z, core))

            group(1, XY, make, l2z.at[it, pl.ds(1, XY - 1)], *send)
        else:
            arrived(l1.at[it, t, pl.ds(1, XY - 1)], *sems)
            value = s1[it, t, sec, rows(g, BLOCK), :].astype(F32)
            for d in range(1, XY):
                value = value + l1[it, t, d].astype(F32)
            s2[it, t] = value.astype(BF16)

            def make(d):
                zz = rem(z + d, Z)
                return copy(s2.at[it, t, rows(zz, CHUNK)], l2.at[it, t, d], *send, at(x, y, zz, core))

            group(1, Z, make, l2.at[it, t, pl.ds(1, Z - 1)], *send)

    def z_copies(ref, sems):
        return lambda d: copy(ref, ref, *sems, at(x, y, rem(z + d, Z), core))

    def g_copies(ref, sems):
        def make(d):
            xx, yy = g_to(d)
            return copy(ref, ref, *sems, at(xx, yy, z, core))

        return make

    def reduce_second(it, t):
        sems = s2_s.at[it, t], s2_r.at[it, t]
        if t == LAST:
            arrived(l2z.at[it, pl.ds(1, XY - 1)], *sems)
            value = s2z[it, sec, rows(g, CHUNK), :].astype(F32)
            for d in range(1, XY):
                value = value + l2z[it, d].astype(F32)
        else:
            arrived(l2.at[it, t, pl.ds(1, Z - 1)], *sems)
            value = s2[it, t, rows(z, CHUNK), :].astype(F32)
            for d in range(1, Z):
                value = value + l2[it, t, d].astype(F32)
        size = sizes[first + t]
        begin = own[t] * CHUNK
        r = lax.broadcasted_iota(jnp.int32, (CHUNK, 128), 0) + rem(begin, M)
        q = lax.broadcasted_iota(jnp.int32, (CHUNK, 128), 1) + (2 * core + div(begin, M)) * 128
        factor = steps[it].astype(F32) * (1.0 / (8.0 * math.sqrt(OPERATORS)))
        value = jnp.where((r < size) & (q < size), chunk[t] - factor * value, 0.0)
        chunk[t] = value
        psi[it + 1, t, core, rows(own[t], CHUNK), :] = value.astype(BF16)
        ref = psi.at[it + 1, t, core, rows(own[t], CHUNK)]
        send = a_s.at[it, t], a_r.at[it, t]
        whole = psi.at[it + 1, t, core, pl.ds(0, 7 * CHUNK)]
        group(1, 8, (g_copies if t == LAST else z_copies)(ref, send), whole, *send)

    def gather_second(it, t):
        arrived(psi.at[it + 1, t, core, pl.ds(0, 7 * CHUNK)], a_s.at[it, t], a_r.at[it, t])
        ref = psi.at[it + 1, t, core, rows(z if t == LAST else g, BLOCK)]
        send = b_s.at[it, t], b_r.at[it, t]
        if it == 1 and t == 0:
            src = psi.at[2, 0, core, rows(g, BLOCK)]
            dst = bas.at[core, rows(g, BLOCK)]

            def make(d):
                xx, yy = xy_to(rem(d, X) + X * (2 * div(d, X) + 1))
                return copy(src, dst, bas_s.at[0], bas_r.at[0], at(xx, yy, z, core))

            @pl.when(sec == 0)
            def _():
                loop(0, G, lambda d: make(d).start())

            @sent.append
            def _():
                @pl.when(sec == 0)
                def _():
                    copy(bas.at[0], bas.at[0], bas_s.at[0], bas_r.at[0], partner).wait_send()

        whole = psi.at[it + 1, t, core, pl.ds(0, 7 * BLOCK)]
        group(1, 8, (z_copies if t == LAST else g_copies)(ref, send), whole, *send)

    def forward_copy(it, t):
        ref = psi.at[it + 1, t, core]
        return copy(ref, ref, f_s.at[it, t], f_r.at[it, t], partner)

    def forward(it, t):
        arrived(psi.at[it + 1, t, core, pl.ds(0, 7 * BLOCK)], b_s.at[it, t], b_r.at[it, t])
        start(forward_copy(it, t))

    def norm_z(it):
        value = jnp.zeros((8, 128), F32)
        for t in range(4):
            part = chunk[t]
            value = value + jnp.sum((part * part).reshape(CHUNK // 8, 8, 128), axis=0)
        nz[it, 0] = value
        sems = n_s.at[it, 0], n_r.at[it, 0]

        def make(d):
            return copy(nz.at[it, 0], nz.at[it, d], *sems, at(x, y, rem(z + d, Z), core))

        group(1, Z, make, nz.at[it, pl.ds(1, Z - 1)], *sems)

    def norm_xy(it):
        arrived(nz.at[it, pl.ds(1, Z - 1)], n_s.at[it, 0], n_r.at[it, 0])
        nxy[it, 0] = jnp.sum(nz[it], axis=0)
        sems = n_s.at[it, 1], n_r.at[it, 1]

        def make(d):
            xx, yy = xy_to(d)
            return copy(nxy.at[it, 0], nxy.at[it, d], *sems, at(xx, yy, z, core))

        group(1, XY, make, nxy.at[it, pl.ds(1, XY - 1)], *sems)

    def norm_copy(it):
        return copy(nc.at[it, 0], nc.at[it, 1], n_s.at[it, 2], n_r.at[it, 2], partner)

    def norm_core(it):
        arrived(nxy.at[it, pl.ds(1, XY - 1)], n_s.at[it, 1], n_r.at[it, 1])
        nc[it, 0] = jnp.sum(nxy[it], axis=0)
        start(norm_copy(it))

    def norm_end(it):
        norm_copy(it).wait_recv()
        total[it] = nc[it, 0] + nc[it, 1]

    near_copies = [
        copy(left.at[0], near.at[0], near_s.at[0], near_r.at[0], after),
        copy(left.at[0], near.at[1], near_s.at[1], near_r.at[1], before),
    ]

    def mix():
        for c in near_copies:
            c.wait_recv()
        w0 = jnp.where(ops == 0, 0.0, integ[0, 0])
        w1 = integ[0, 1]
        w2 = jnp.where(ops == OPERATORS - 1, 0.0, integ[0, 2])

        def body(i):
            part = rows(i, 64)
            lmix[part, :] = (
                w0 * near[0, part, :].astype(F32)
                + w1 * left[0, part, :].astype(F32)
                + w2 * near[1, part, :].astype(F32)
            ).astype(BF16)

        loop(0, M // 64, body)

    def write_wave(t):
        for b in range(4):
            psi_out[t, :, 128 * b : 128 * b + 128] = psi[2, t, b // 2, pl.ds(b % 2 * M, M), :]
        made = pltpu.make_async_copy(psi_out.at[t], psi_hbm.at[t], out_s.at[t])
        made.start()
        sent.append(made.wait)

    bas_copy = copy(bas.at[core], bas.at[core], bas_s.at[1], bas_r.at[1], partner)

    def basis_forward():
        @pl.when(sec == 1)
        def _():
            arrived(bas.at[core], bas_s.at[0], bas_r.at[0])
            bas_copy.start()

        @sent.append
        def _():
            @pl.when(sec == 1)
            def _():
                bas_copy.wait_send()

    def rotate():
        @pl.when(sec == 0)
        def _():
            bas[...] = psi[2, 0]

        @pl.when(sec == 1)
        def _():
            bas_copy.wait_recv()

        basis_cols = jnp.concatenate([bas[sec, pl.ds(b * M, M), :] for b in range(2)], axis=1)
        half = jnp.dot(lmix[...], basis_cols, preferred_element_type=F32).astype(BF16)
        rotated[...] = lax.dot_general(
            columns(bas), half, (((0,), (0,)), ((), ())), preferred_element_type=F32
        )

    shift_copy = copy(shifts.at[0], shifts.at[1], sh_s.at[0], sh_r.at[0], partner)
    for s in range(4):
        compute(0, s)
        if s == 1:
            pl.semaphore_wait(barrier, 3 + XY - 1 + Z - 1)
            start(shift_copy)
            exchange(0, 0)
            exchange(0, 1)
    shift_copy.wait_recv()
    for it in range(2):
        for s in (0, 1, 3, 2):
            core_copy(it, s).wait_recv()
        for t in ORDER:
            scatter(it, t)
            if it == 1 and t == LAST:
                for c in near_copies:
                    start(c)
        if it == 1:
            norm_z(0)
        reduce_first(it, 0)
        reduce_first(it, 3)
        reduce_first(it, 1)
        if it == 1:
            norm_xy(0)
        reduce_second(it, 0)
        reduce_first(it, 2)
        reduce_second(it, 3)
        reduce_second(it, 1)
        gather_second(it, 0)
        reduce_second(it, 2)
        if it == 1:
            norm_z(1)
        gather_second(it, 1)
        gather_second(it, 3)
        if it == 1:
            norm_core(0)
            mix()
        forward(it, 0)
        if it == 1:
            basis_forward()
        if it == 1:
            norm_xy(1)
        gather_second(it, 2)
        forward(it, 1)
        forward_copy(it, 0).wait_recv()
        if it == 0:
            compute(1, 0)
        else:
            write_wave(0)
            rotate()
        forward_copy(it, 1).wait_recv()
        if it == 0:
            compute(1, 1)
        else:
            write_wave(1)
        forward(it, 3)
        forward(it, 2)
        if it == 1:
            norm_core(1)
        for t in (3, 2):
            forward_copy(it, t).wait_recv()
            if it == 0:
                compute(1, t)
            else:
                write_wave(t)
    norm_end(0)
    norm_end(1)

    count = float(S * M * M)
    sum1 = jnp.sum(total[0], axis=(0, 1), keepdims=True)
    sum2 = jnp.sum(total[1], axis=(0, 1), keepdims=True)
    square = sum2 * (1.0 / count) + 1e-06 * (sum1 * (1.0 / count) + 1e-06)
    scale = lax.rsqrt(square)
    scale_out[...] = jnp.broadcast_to(scale, (1, M))
    mixed_out[0] = (rotated[...] * (scale * scale * (1.0 / M))).astype(BF16)

    for wait in sent:
        wait()


def shards(*args):
    vmem = pl.BlockSpec(memory_space=pltpu.VMEM)
    smem = pl.BlockSpec(memory_space=pltpu.SMEM)
    hbm = pl.BlockSpec(memory_space=pltpu.HBM)

    def low(*shape):
        return pltpu.VMEM(shape, BF16)

    def full(*shape):
        return pltpu.VMEM(shape, F32)

    def pair(*shape):
        return [pltpu.SemaphoreType.DMA(shape)] * 2

    wave, mixed, scale = pl.pallas_call(
        kernel,
        out_shape=(
            jax.ShapeDtypeStruct((4, M, M), BF16),
            jax.ShapeDtypeStruct((1, M, M // 2), BF16),
            jax.ShapeDtypeStruct((1, M), F32),
        ),
        in_specs=[hbm, hbm, hbm, hbm, smem, smem, smem],
        out_specs=(hbm, vmem, vmem),
        scratch_shapes=[
            low(4, M, M),
            low(1, M, M),
            low(1, M, M),
            pltpu.SMEM((1,), jnp.int32),
            low(4, M, M),
            low(3, 4, 2, HALF, 128),
            low(2, HALF, 128),
            low(2, M, 256),
            low(2, M, M),
            low(M, M),
            full(4, CHUNK, 128),
            full(4, HALF, 128),
            pltpu.SMEM((2, 1), jnp.int32),
            low(2, 4, HALF, 128),
            low(2, 4, HALF, 128),
            low(2, 4, 2, HALF, 128),
            low(2, 3, XY, BLOCK, 128),
            low(2, Z, 2, BLOCK, 128),
            low(2, 3, BLOCK, 128),
            low(2, 2, BLOCK, 128),
            low(2, 3, Z, CHUNK, 128),
            low(2, XY, CHUNK, 128),
            full(2, Z, 8, 128),
            full(2, XY, 8, 128),
            full(2, 2, 8, 128),
            full(2, 8, 128),
            full(M, M // 2),
            *pair(2),
            *pair(2, 4),
            *pair(2, 4),
            *pair(2, 4),
            *pair(2, 4),
            *pair(2, 4),
            *pair(2, 4),
            *pair(2),
            *pair(2, 3),
            *pair(1),
            pltpu.SemaphoreType.DMA((7,)),
            pltpu.SemaphoreType.DMA((4,)),
        ],
        compiler_params=pltpu.CompilerParams(
            collective_id=0, has_side_effects=True, vmem_limit_bytes=60 * 2**20
        ),
        name="dmrg_window",
    )(*args)
    return wave.astype(F32) * scale, mixed


def solution(mesh):
    placed = (
        P("sec", None, None),
        P("ops", None, None),
        P("ops", None, None),
        P("ops"),
        P(),
        P(),
        P("ops", None),
    )
    return jax.shard_map(
        shards,
        mesh=mesh,
        in_specs=placed,
        out_specs=(P("sec", None, None), P("ops", None, "sec")),
        check_vma=False,
    )
```

```python
import math

import jax
import jax.numpy as jnp
from jax import lax
from jax.experimental import pallas as pl
from jax.experimental.pallas import tpu as pltpu
from jax.sharding import PartitionSpec as P

MESH = pl.DeviceIdType.MESH
F32 = jnp.float32
BF16 = jnp.bfloat16
M = 512
S = 8
OPERATORS = 128
YH, X, Z = 2, 4, 8
G = YH * X
Y = 2 * YH
XY = X * Y
HALF = 2 * M
CHUNK = HALF // (G * Z)
BLOCK = HALF // 8
LAST = 3
ORDER = (0, 3, 1, 2)


def loop(low, high, body):
    lax.fori_loop(low, high, lambda i, c: (body(i), c)[1], 0)


def rem(a, b):
    return lax.rem(a, jnp.int32(b))


def div(a, b):
    return lax.div(a, jnp.int32(b))


def rows(o, n):
    return pl.ds(pl.multiple_of(o * n, n), n)


def kernel(
    wave_hbm, left_hbm, right_hbm, shift_hbm, sizes, steps, integ,
    psi_out, mixed_out, scale_out,
    wave, left, right, shift, psi, bas, right_t, near, lmix, chunk, acc,
    shifts, csend, cland, s1, l1, l1z, s2, s2z, l2, l2z, nz, nxy, nc, total, rotated,
    near_s, near_r, c_s, c_r, s1_s, s1_r, s2_s, s2_r, a_s, a_r, b_s, b_r, f_s, f_r, bas_s, bas_r, n_s, n_r, sh_s, sh_r, in_s,
):
    ops = lax.axis_index("ops")
    sec = lax.axis_index("sec")
    core = rem(ops, 2)
    z = rem(div(ops, 2), Z)
    x = rem(div(ops, 2 * Z), X)
    yh = div(ops, 2 * Z * X)
    y = yh * 2 + sec
    g = yh * X + x
    first = sec * 4

    def at(xx, yy, zz, cc):
        return ((div(yy, 2) * X + xx) * Z + zz) * 2 + cc, rem(yy, 2)

    def xy_to(d):
        return rem(x + rem(d, X), X), rem(y + div(d, X), Y)

    def g_to(d):
        return rem(x + rem(d, X), X), rem(y + 2 * div(d, X), Y)

    partner = at(x, y, z, 1 - core)
    after = (rem(ops + 1, OPERATORS), sec)
    before = (rem(ops + OPERATORS - 1, OPERATORS), sec)

    def copy(src, dst, send, recv, device):
        return pltpu.make_async_remote_copy(
            src_ref=src, dst_ref=dst, send_sem=send, recv_sem=recv, device_id=device, device_id_type=MESH
        )

    sent = []

    def start(made):
        made.start()
        sent.append(made.wait_send)

    def group(low, high, make, whole, send, recv):
        if high - low < XY:
            for d in range(low, high):
                make(jnp.int32(d)).start()
        else:
            loop(low, high, lambda d: make(d).start())
        sent.append(copy(whole, whole, send, recv, partner).wait_send)

    def arrived(whole, send, recv):
        copy(whole, whole, send, recv, partner).wait_recv()

    inputs = [pltpu.make_async_copy(wave_hbm.at[t], wave.at[t], in_s.at[t]) for t in range(4)]
    inputs.append(pltpu.make_async_copy(left_hbm, left, in_s.at[4]))
    inputs.append(pltpu.make_async_copy(right_hbm, right, in_s.at[5]))
    inputs.append(pltpu.make_async_copy(shift_hbm, shift, in_s.at[6]))
    for t in (6, 0, 5, 4, 1, 2, 3):
        inputs[t].start()

    barrier = pltpu.get_barrier_semaphore()

    def greet(device):
        pl.semaphore_signal(barrier, inc=1, device_id=device, device_id_type=MESH)

    greet(after)
    greet(before)

    def greet_xy(d):
        xx, yy = xy_to(d)
        greet(at(xx, yy, z, core))

    loop(1, XY, greet_xy)
    loop(1, Z, lambda d: greet(at(x, y, rem(z + d, Z), core)))
    greet(partner)

    row = lax.broadcasted_iota(jnp.int32, (M, 128), 0)
    col = lax.broadcasted_iota(jnp.int32, (M, 128), 1)

    def fill(t):
        size = sizes[first + t]
        for b in range(4):
            ok = (row < size) & (col < size - 128 * b)
            block = wave[t, :, 128 * b : 128 * b + 128].astype(F32)
            psi[0, t, b // 2, pl.ds(b % 2 * M, M), :] = jnp.where(ok, block, 0.0).astype(BF16)

    inputs[6].wait()
    shifts[0, 0] = shift[0]
    for t in range(4):
        inputs[t].wait()
        fill(t)
    inputs[5].wait()
    for h in range(2):
        right_t[h] = right[0, 256 * h : 256 * h + 256, :].T
    own = [z * G + g if t == LAST else g * Z + z for t in range(4)]
    for t in range(4):
        chunk[t] = psi[0, t, core, rows(own[t], CHUNK), :].astype(F32)

    inputs[4].wait()

    def columns(ref):
        return jnp.concatenate([ref[b // 2, pl.ds(b % 2 * M, M), :] for b in range(4)], axis=1)

    def compute(it, s):
        inner = jnp.dot(left[0], columns(psi.at[it, s]), preferred_element_type=F32).astype(BF16)
        theirs = jnp.dot(inner, right_t[1 - core], preferred_element_type=F32).astype(BF16)
        csend[it, s, pl.ds(0, M), :] = theirs[:, :128]
        csend[it, s, pl.ds(M, M), :] = theirs[:, 128:]
        if it or s > 1:
            exchange(it, s)
        mine = jnp.dot(inner, right_t[core], preferred_element_type=F32)
        acc[s, pl.ds(0, M), :] = mine[:, :128]
        acc[s, pl.ds(M, M), :] = mine[:, 128:]

    def source(a, t, by):
        s = rem(a * 4 + t - first - by + 2 * S, S)
        return jnp.minimum(s, 3), jnp.where(s < 4, 1.0, 0.0).astype(F32)

    def core_copy(it, t):
        return copy(csend.at[it, t], cland.at[it, t], c_s.at[it, t], c_r.at[it, t], partner)

    def exchange(it, s):
        start(core_copy(it, s))

    def scatter(it, t):
        for a in range(2):
            s, gate = source(a, t, shift[0])
            ps, pgate = source(a, t, shifts[1, 0])
            for b in range(4):
                part = pl.ds(256 * b, 256)
                s1[it, t, a, part, :] = (
                    acc[s, part, :] * gate + cland[it, ps, part, :].astype(F32) * pgate
                ).astype(BF16)
        sems = s1_s.at[it, t], s1_r.at[it, t]
        if t == LAST:

            def make(d):
                zz = rem(z + d, Z)
                return copy(s1.at[it, t, :, rows(zz, BLOCK)], l1z.at[it, d], *sems, at(x, y, zz, core))

            group(1, Z, make, l1z.at[it, pl.ds(1, Z - 1)], *sems)
        else:

            def make(d):
                xx, yy = xy_to(d)
                src = s1.at[it, t, rem(yy, 2), rows(div(yy, 2) * X + xx, BLOCK)]
                return copy(src, l1.at[it, t, d], *sems, at(xx, yy, z, core))

            group(1, XY, make, l1.at[it, t, pl.ds(1, XY - 1)], *sems)

    def reduce_first(it, t):
        sems = s1_s.at[it, t], s1_r.at[it, t]
        send = s2_s.at[it, t], s2_r.at[it, t]
        if t == LAST:
            arrived(l1z.at[it, pl.ds(1, Z - 1)], *sems)
            for a in range(2):
                value = s1[it, t, a, rows(z, BLOCK), :].astype(F32)
                for d in range(1, Z):
                    value = value + l1z[it, d, a].astype(F32)
                s2z[it, a] = value.astype(BF16)

            def make(d):
                xx, yy = xy_to(d)
                src = s2z.at[it, rem(yy, 2), rows(div(yy, 2) * X + xx, CHUNK)]
                return copy(src, l2z.at[it, d], *send, at(xx, yy, z, core))

            group(1, XY, make, l2z.at[it, pl.ds(1, XY - 1)], *send)
        else:
            arrived(l1.at[it, t, pl.ds(1, XY - 1)], *sems)
            value = s1[it, t, sec, rows(g, BLOCK), :].astype(F32)
            for d in range(1, XY):
                value = value + l1[it, t, d].astype(F32)
            s2[it, t] = value.astype(BF16)

            def make(d):
                zz = rem(z + d, Z)
                return copy(s2.at[it, t, rows(zz, CHUNK)], l2.at[it, t, d], *send, at(x, y, zz, core))

            group(1, Z, make, l2.at[it, t, pl.ds(1, Z - 1)], *send)

    def z_copies(ref, sems):
        return lambda d: copy(ref, ref, *sems, at(x, y, rem(z + d, Z), core))

    def g_copies(ref, sems):
        def make(d):
            xx, yy = g_to(d)
            return copy(ref, ref, *sems, at(xx, yy, z, core))

        return make

    def reduce_second(it, t):
        sems = s2_s.at[it, t], s2_r.at[it, t]
        if t == LAST:
            arrived(l2z.at[it, pl.ds(1, XY - 1)], *sems)
            value = s2z[it, sec, rows(g, CHUNK), :].astype(F32)
            for d in range(1, XY):
                value = value + l2z[it, d].astype(F32)
        else:
            arrived(l2.at[it, t, pl.ds(1, Z - 1)], *sems)
            value = s2[it, t, rows(z, CHUNK), :].astype(F32)
            for d in range(1, Z):
                value = value + l2[it, t, d].astype(F32)
        size = sizes[first + t]
        begin = own[t] * CHUNK
        r = lax.broadcasted_iota(jnp.int32, (CHUNK, 128), 0) + rem(begin, M)
        q = lax.broadcasted_iota(jnp.int32, (CHUNK, 128), 1) + (2 * core + div(begin, M)) * 128
        factor = steps[it].astype(F32) * (1.0 / (8.0 * math.sqrt(OPERATORS)))
        value = jnp.where((r < size) & (q < size), chunk[t] - factor * value, 0.0)
        chunk[t] = value
        psi[it + 1, t, core, rows(own[t], CHUNK), :] = value.astype(BF16)
        ref = psi.at[it + 1, t, core, rows(own[t], CHUNK)]
        send = a_s.at[it, t], a_r.at[it, t]
        whole = psi.at[it + 1, t, core, pl.ds(0, 7 * CHUNK)]
        group(1, 8, (g_copies if t == LAST else z_copies)(ref, send), whole, *send)

    def gather_second(it, t):
        arrived(psi.at[it + 1, t, core, pl.ds(0, 7 * CHUNK)], a_s.at[it, t], a_r.at[it, t])
        ref = psi.at[it + 1, t, core, rows(z if t == LAST else g, BLOCK)]
        send = b_s.at[it, t], b_r.at[it, t]
        if it == 1 and t == 0:
            src = psi.at[2, 0, core, rows(g, BLOCK)]
            dst = bas.at[core, rows(g, BLOCK)]

            def make(d):
                xx, yy = xy_to(rem(d, X) + X * (2 * div(d, X) + 1))
                return copy(src, dst, bas_s.at[0], bas_r.at[0], at(xx, yy, z, core))

            @pl.when(sec == 0)
            def _():
                loop(0, G, lambda d: make(d).start())

            @sent.append
            def _():
                @pl.when(sec == 0)
                def _():
                    copy(bas.at[0], bas.at[0], bas_s.at[0], bas_r.at[0], partner).wait_send()

        whole = psi.at[it + 1, t, core, pl.ds(0, 7 * BLOCK)]
        group(1, 8, (z_copies if t == LAST else g_copies)(ref, send), whole, *send)

    def forward_copy(it, t):
        ref = psi.at[it + 1, t, core]
        return copy(ref, ref, f_s.at[it, t], f_r.at[it, t], partner)

    def forward(it, t):
        arrived(psi.at[it + 1, t, core, pl.ds(0, 7 * BLOCK)], b_s.at[it, t], b_r.at[it, t])
        start(forward_copy(it, t))

    def norm_z(it):
        value = jnp.zeros((8, 128), F32)
        for t in range(4):
            part = chunk[t]
            value = value + jnp.sum((part * part).reshape(CHUNK // 8, 8, 128), axis=0)
        nz[it, 0] = value
        sems = n_s.at[it, 0], n_r.at[it, 0]

        def make(d):
            return copy(nz.at[it, 0], nz.at[it, d], *sems, at(x, y, rem(z + d, Z), core))

        group(1, Z, make, nz.at[it, pl.ds(1, Z - 1)], *sems)

    def norm_xy(it):
        arrived(nz.at[it, pl.ds(1, Z - 1)], n_s.at[it, 0], n_r.at[it, 0])
        nxy[it, 0] = jnp.sum(nz[it], axis=0)
        sems = n_s.at[it, 1], n_r.at[it, 1]

        def make(d):
            xx, yy = xy_to(d)
            return copy(nxy.at[it, 0], nxy.at[it, d], *sems, at(xx, yy, z, core))

        group(1, XY, make, nxy.at[it, pl.ds(1, XY - 1)], *sems)

    def norm_copy(it):
        return copy(nc.at[it, 0], nc.at[it, 1], n_s.at[it, 2], n_r.at[it, 2], partner)

    def norm_core(it):
        arrived(nxy.at[it, pl.ds(1, XY - 1)], n_s.at[it, 1], n_r.at[it, 1])
        nc[it, 0] = jnp.sum(nxy[it], axis=0)
        start(norm_copy(it))

    def norm_end(it):
        norm_copy(it).wait_recv()
        total[it] = nc[it, 0] + nc[it, 1]

    near_copies = [
        copy(left.at[0], near.at[0], near_s.at[0], near_r.at[0], after),
        copy(left.at[0], near.at[1], near_s.at[1], near_r.at[1], before),
    ]

    def mix():
        for c in near_copies:
            c.wait_recv()
        w0 = jnp.where(ops == 0, 0.0, integ[0, 0])
        w1 = integ[0, 1]
        w2 = jnp.where(ops == OPERATORS - 1, 0.0, integ[0, 2])

        def body(i):
            part = rows(i, 64)
            lmix[part, :] = (
                w0 * near[0, part, :].astype(F32)
                + w1 * left[0, part, :].astype(F32)
                + w2 * near[1, part, :].astype(F32)
            ).astype(BF16)

        loop(0, M // 64, body)

    def write_wave(t):
        for b in range(4):
            psi_out[t, :, 128 * b : 128 * b + 128] = psi[2, t, b // 2, pl.ds(b % 2 * M, M), :]

    bas_copy = copy(bas.at[core], bas.at[core], bas_s.at[1], bas_r.at[1], partner)

    def basis_forward():
        @pl.when(sec == 1)
        def _():
            arrived(bas.at[core], bas_s.at[0], bas_r.at[0])
            bas_copy.start()

        @sent.append
        def _():
            @pl.when(sec == 1)
            def _():
                bas_copy.wait_send()

    def rotate():
        @pl.when(sec == 0)
        def _():
            bas[...] = psi[2, 0]

        @pl.when(sec == 1)
        def _():
            bas_copy.wait_recv()

        basis_cols = jnp.concatenate([bas[sec, pl.ds(b * M, M), :] for b in range(2)], axis=1)
        half = jnp.dot(lmix[...], basis_cols, preferred_element_type=F32).astype(BF16)
        rotated[...] = lax.dot_general(
            columns(bas), half, (((0,), (0,)), ((), ())), preferred_element_type=F32
        )

    shift_copy = copy(shifts.at[0], shifts.at[1], sh_s.at[0], sh_r.at[0], partner)
    for s in range(4):
        compute(0, s)
        if s == 1:
            pl.semaphore_wait(barrier, 3 + XY - 1 + Z - 1)
            start(shift_copy)
            exchange(0, 0)
            exchange(0, 1)
    shift_copy.wait_recv()
    for it in range(2):
        for s in (0, 1, 3, 2):
            core_copy(it, s).wait_recv()
        for t in ORDER:
            scatter(it, t)
            if it == 1 and t == LAST:
                for c in near_copies:
                    start(c)
        if it == 1:
            norm_z(0)
        reduce_first(it, 0)
        reduce_first(it, 3)
        reduce_first(it, 1)
        if it == 1:
            norm_xy(0)
        reduce_second(it, 0)
        reduce_first(it, 2)
        reduce_second(it, 3)
        reduce_second(it, 1)
        gather_second(it, 0)
        reduce_second(it, 2)
        if it == 1:
            norm_z(1)
        gather_second(it, 1)
        gather_second(it, 3)
        if it == 1:
            norm_core(0)
            mix()
        forward(it, 0)
        if it == 1:
            basis_forward()
        if it == 1:
            norm_xy(1)
        gather_second(it, 2)
        forward(it, 1)
        forward_copy(it, 0).wait_recv()
        if it == 0:
            compute(1, 0)
        else:
            write_wave(0)
            rotate()
        forward_copy(it, 1).wait_recv()
        if it == 0:
            compute(1, 1)
        else:
            write_wave(1)
        forward(it, 3)
        forward(it, 2)
        if it == 1:
            norm_core(1)
        for t in (3, 2):
            forward_copy(it, t).wait_recv()
            if it == 0:
                compute(1, t)
            else:
                write_wave(t)
    norm_end(0)
    norm_end(1)

    count = float(S * M * M)
    sum1 = jnp.sum(total[0], axis=(0, 1), keepdims=True)
    sum2 = jnp.sum(total[1], axis=(0, 1), keepdims=True)
    square = sum2 * (1.0 / count) + 1e-06 * (sum1 * (1.0 / count) + 1e-06)
    scale = lax.rsqrt(square)
    scale_out[...] = jnp.broadcast_to(scale, (1, M))
    mixed_out[0] = (rotated[...] * (scale * scale * (1.0 / M))).astype(BF16)

    for wait in sent:
        wait()


def shards(*args):
    vmem = pl.BlockSpec(memory_space=pltpu.VMEM)
    smem = pl.BlockSpec(memory_space=pltpu.SMEM)
    hbm = pl.BlockSpec(memory_space=pltpu.HBM)

    def low(*shape):
        return pltpu.VMEM(shape, BF16)

    def full(*shape):
        return pltpu.VMEM(shape, F32)

    def pair(*shape):
        return [pltpu.SemaphoreType.DMA(shape)] * 2

    wave, mixed, scale = pl.pallas_call(
        kernel,
        out_shape=(
            jax.ShapeDtypeStruct((4, M, M), BF16),
            jax.ShapeDtypeStruct((1, M, M // 2), BF16),
            jax.ShapeDtypeStruct((1, M), F32),
        ),
        in_specs=[hbm, hbm, hbm, hbm, smem, smem, smem],
        out_specs=(vmem, vmem, vmem),
        scratch_shapes=[
            low(4, M, M),
            low(1, M, M),
            low(1, M, M),
            pltpu.SMEM((1,), jnp.int32),
            low(3, 4, 2, HALF, 128),
            low(2, HALF, 128),
            low(2, M, 256),
            low(2, M, M),
            low(M, M),
            full(4, CHUNK, 128),
            full(4, HALF, 128),
            pltpu.SMEM((2, 1), jnp.int32),
            low(2, 4, HALF, 128),
            low(2, 4, HALF, 128),
            low(2, 4, 2, HALF, 128),
            low(2, 3, XY, BLOCK, 128),
            low(2, Z, 2, BLOCK, 128),
            low(2, 3, BLOCK, 128),
            low(2, 2, BLOCK, 128),
            low(2, 3, Z, CHUNK, 128),
            low(2, XY, CHUNK, 128),
            full(2, Z, 8, 128),
            full(2, XY, 8, 128),
            full(2, 2, 8, 128),
            full(2, 8, 128),
            full(M, M // 2),
            *pair(2),
            *pair(2, 4),
            *pair(2, 4),
            *pair(2, 4),
            *pair(2, 4),
            *pair(2, 4),
            *pair(2, 4),
            *pair(2),
            *pair(2, 3),
            *pair(1),
            pltpu.SemaphoreType.DMA((7,)),
        ],
        compiler_params=pltpu.CompilerParams(
            collective_id=0, has_side_effects=True, vmem_limit_bytes=60 * 2**20
        ),
        name="dmrg_window",
    )(*args)
    return wave.astype(F32) * scale, mixed


def solution(mesh):
    placed = (
        P("sec", None, None),
        P("ops", None, None),
        P("ops", None, None),
        P("ops"),
        P(),
        P(),
        P("ops", None),
    )
    return jax.shard_map(
        shards,
        mesh=mesh,
        in_specs=placed,
        out_specs=(P("sec", None, None), P("ops", None, "sec")),
        check_vma=False,
    )
```
